512 devices in a mesh: dp: 256 (over y, x, z), ctx: 2 (over core).
Axes of the slice: x: 4, y: 4, z: 16, core: 2. Of those that a mesh axis runs over, the one named last changes fastest.
Arguments:
- q_weight: bfloat16 [256, 256, 2, 576], P(None, 'dp', 'ctx'), may hold values from -6 to 6
- kv_weight: bfloat16 [256, 256, 2, 256], P(None, 'dp', 'ctx'), may hold values from -6 to 6
- q_grad: bfloat16 [2, 256, 256, 2, 576], P('ctx', None, 'dp'), may hold values from -6 to 6
- kv_grad: bfloat16 [2, 256, 256, 2, 256], P('ctx', None, 'dp'), may hold values from -6 to 6
- q_moment: float32 [256, 2, 256, 576], P(None, 'ctx', 'dp')
- kv_moment: float32 [256, 2, 256, 256], P(None, 'ctx', 'dp')
- logit_part: float32 [256, 2, 256], P('dp', 'ctx'), may hold values from 5 to 300, as said below
- slot_table: int32 [256], replicated, may hold values from 0 to 255, each once
Outputs:
- q_weight_out: bfloat16 [256, 256, 2, 576], P(None, 'dp', 'ctx')
- kv_weight_out: bfloat16 [256, 256, 2, 256], P(None, 'dp', 'ctx')
- q_moment_out: float32 [256, 2, 256, 576], P(None, 'ctx', 'dp')
- kv_moment_out: float32 [256, 2, 256, 256], P(None, 'ctx', 'dp')
The draws below stay inside these ranges and needn't reach their ends.
Inputs may be any that keep to these rules, and one draw needn't show every extreme that they name: `slot_table`: a permutation; the block in slot s is owned by index s // 1 of dp. `logit_part`: positive.
All inputs are finite; a program needn't handle non-finite values.
Results may differ from the reference program's by a relative error of at most 0.023.
Values may be sent and summed in bfloat16 or wider, within the bound.
A program may use at most 64 MiB of HBM per device.

```python
import math
import jax
import jax.numpy as jnp
from jax import lax

QRANK = 1536
KVRANK = 512
NOPE = 128
ITERS = 5
QDIM = 192
KVDIM = 256
PAIRS = 256
QR_DEV = 3
KVR_DEV = 1
N_DP = 256
N_CTX = 2


def scale_field(key, row_shape, col_shape, lowest, highest):
    row_key, col_key = jax.random.split(key)
    rows = jnp.exp(jax.random.uniform(row_key, row_shape, jnp.float32, jnp.log(lowest), jnp.log(highest)))
    cols = jnp.exp(jax.random.uniform(col_key, col_shape, jnp.float32, jnp.log(lowest), jnp.log(highest)))
    return rows * cols


def draw_q_moment(key, part):
    key = jax.random.fold_in(key, 11)
    base_key, scale_key = jax.random.split(key)
    shape = (N_DP, N_CTX, PAIRS, QR_DEV, QDIM)
    base = jax.random.normal(base_key, shape, jnp.float32)
    field = scale_field(scale_key, (N_DP, N_CTX, PAIRS, QR_DEV, 1), (1, 1, PAIRS, 1, QDIM), 0.3, 3.0)
    return (base * field).reshape(N_DP, N_CTX, PAIRS, QR_DEV * QDIM)


def draw_kv_moment(key, part):
    key = jax.random.fold_in(key, 17)
    base_key, scale_key = jax.random.split(key)
    shape = (N_DP, N_CTX, PAIRS, KVR_DEV, KVDIM)
    base = jax.random.normal(base_key, shape, jnp.float32)
    field = scale_field(scale_key, (N_DP, N_CTX, PAIRS, KVR_DEV, 1), (1, 1, PAIRS, 1, KVDIM), 0.3, 3.0)
    return (base * field).reshape(N_DP, N_CTX, PAIRS, KVR_DEV * KVDIM)


def draw_logit_part(key, part):
    key = jax.random.fold_in(key, 29)
    level_key, lead_key, share_key = jax.random.split(key, 3)
    holders = N_DP * N_CTX
    level = jnp.exp(jax.random.uniform(level_key, (PAIRS,), jnp.float32, jnp.log(60.0), jnp.log(300.0)))
    share = jax.random.uniform(share_key, (holders, PAIRS), jnp.float32, 0.2, 0.6)
    leader = jax.random.randint(lead_key, (PAIRS,), 0, holders)
    chosen = jnp.arange(holders)[:, None] == leader[None, :]
    values = jnp.where(chosen, 1.0, share) * level[None, :]
    return values.reshape(N_DP, N_CTX, PAIRS)


def shard_levels(rng, dims, pieces, smallest, largest):
    level = 1.0
    for position, parts in pieces:
        steps = jax.random.uniform(jax.random.fold_in(jax.random.fold_in(rng, 6), position), (parts,), jnp.float32, smallest / len(pieces), largest / len(pieces))
        level = level * jnp.repeat(jnp.exp(steps), dims[position] // parts).reshape((-1,) + (1,) * (len(dims) - 1 - position))
    return level


def normal_values(rng, dims, width, bound, shards=(), held_as=jnp.bfloat16):
    entries = jax.random.normal(rng, dims, jnp.float32) * width
    if len(shards) > 0:
        entries = shard_levels(rng, dims, shards, -0.22, 0.18) * entries
    return jnp.clip(entries, min=-bound, max=bound).astype(held_as)


def setup_inputs(seed: int = 0) -> dict:
    streams_of = jax.random.split(jax.random.key(seed), 9)
    return {
        "q_weight": normal_values(streams_of[0], (PAIRS, N_DP, N_CTX, QR_DEV * QDIM), 1.0, 6.0, ((1, 256), (2, 2))),
        "kv_weight": normal_values(streams_of[1], (PAIRS, N_DP, N_CTX, KVR_DEV * KVDIM), 1.0, 6.0, ((1, 256), (2, 2))),
        "q_grad": normal_values(streams_of[2], (N_CTX, PAIRS, N_DP, N_CTX, QR_DEV * QDIM), 1.0, 6.0, ((0, 2), (2, 256))),
        "kv_grad": normal_values(streams_of[3], (N_CTX, PAIRS, N_DP, N_CTX, KVR_DEV * KVDIM), 1.0, 6.0, ((0, 2), (2, 256))),
        "q_moment": draw_q_moment(jax.random.fold_in(streams_of[8], 71), 0),
        "kv_moment": draw_kv_moment(jax.random.fold_in(streams_of[8], 71), 0),
        "logit_part": draw_logit_part(jax.random.fold_in(streams_of[8], 71), 0),
        "slot_table": jax.random.permutation(streams_of[7], PAIRS).astype(jnp.int32),
    }


newton_a = 3.4445
newton_b = -4.775
newton_c = 2.0315
momentum_rate = 0.95
learn_rate = 2.0
weight_decay = 0.1
rms_match = 0.2
clip_limit = 100.0
norm_eps = 1e-06

def normalize(moment):
    total = jnp.sqrt(jnp.sum(moment * moment))
    return (moment / (total + norm_eps)).astype(jnp.bfloat16)

def orthogonalize(blocks):
    states = (normalize(blocks[0]), normalize(blocks[1]))
    for iteration in range(ITERS):
        updated = []
        for state in states:
            gram = jnp.dot(state.T, state, preferred_element_type=jnp.float32).astype(jnp.bfloat16)
            square = jnp.dot(gram, gram, preferred_element_type=jnp.float32)
            mixer = (newton_b * gram.astype(jnp.float32) + newton_c * square).astype(jnp.bfloat16)
            product = jnp.dot(state, mixer, preferred_element_type=jnp.float32)
            updated.append((newton_a * state.astype(jnp.float32) + product).astype(jnp.bfloat16))
        states = (updated[0], updated[1])
    return states

def apply_update(weight, update, clip_cols, rows, cols):
    widened = weight.astype(jnp.float32)
    scale = rms_match * math.sqrt(max(rows, cols))
    fresh = widened - learn_rate * (scale * update.astype(jnp.float32) + weight_decay * widened)
    return (fresh * clip_cols).astype(jnp.bfloat16)

def reference(q_weight, kv_weight, q_grad, kv_grad, q_moment, kv_moment, logit_part, slot_table):
    peak_logit = lax.optimization_barrier(jnp.max(logit_part, axis=(0, 1)))
    clip_factor = jnp.minimum(1.0, clip_limit / peak_logit)
    q_sum = (q_grad[0].astype(jnp.float32) + q_grad[1].astype(jnp.float32)).astype(jnp.bfloat16)
    kv_sum = (kv_grad[0].astype(jnp.float32) + kv_grad[1].astype(jnp.float32)).astype(jnp.bfloat16)
    q_slot = jnp.zeros_like(q_sum).at[slot_table].set(q_sum)
    kv_slot = jnp.zeros_like(kv_sum).at[slot_table].set(kv_sum)
    q_moment_out = momentum_rate * q_moment + jnp.transpose(q_slot, (1, 2, 0, 3)).astype(jnp.float32)
    kv_moment_out = momentum_rate * kv_moment + jnp.transpose(kv_slot, (1, 2, 0, 3)).astype(jnp.float32)
    q_blocks = jnp.transpose(q_moment_out, (2, 0, 1, 3)).reshape(PAIRS, QRANK, QDIM)
    kv_blocks = jnp.transpose(kv_moment_out, (2, 0, 1, 3)).reshape(PAIRS, KVRANK, KVDIM)
    q_final, kv_final = lax.map(orthogonalize, (q_blocks, kv_blocks))
    q_update = q_final[slot_table].reshape(PAIRS, N_DP, N_CTX, QR_DEV, QDIM)
    kv_update = kv_final[slot_table].reshape(PAIRS, N_DP, N_CTX, KVR_DEV, KVDIM)
    root = jnp.sqrt(clip_factor)
    q_cols = jnp.where(jnp.arange(QDIM) < NOPE, root[:, None], clip_factor[:, None])
    kv_cols = jnp.where(jnp.arange(KVDIM) < NOPE, root[:, None], jnp.ones_like(clip_factor)[:, None])
    q_new = apply_update(q_weight.reshape(PAIRS, N_DP, N_CTX, QR_DEV, QDIM), q_update, q_cols[:, None, None, None, :], QRANK, QDIM)
    kv_new = apply_update(kv_weight.reshape(PAIRS, N_DP, N_CTX, KVR_DEV, KVDIM), kv_update, kv_cols[:, None, None, None, :], KVRANK, KVDIM)
    q_weight_out = q_new.reshape(PAIRS, N_DP, N_CTX, QR_DEV * QDIM)
    kv_weight_out = kv_new.reshape(PAIRS, N_DP, N_CTX, KVR_DEV * KVDIM)
    return (q_weight_out, kv_weight_out, q_moment_out, kv_moment_out)
```

```python
import math

import jax
import jax.numpy as jnp
from jax import lax
from jax.experimental import pallas as pl
from jax.experimental.pallas import tpu as pltpu
from jax.sharding import PartitionSpec as P

NOPE = 128
ITERS = 5
QDIM = 192
KVDIM = 256

GY = 4
GX = 4
GZ = 16
GYX = GY * GX
QRANK = 1536
KVRANK = 512

newton_a = 3.4445
newton_b = -4.775
newton_c = 2.0315
momentum_rate = 0.95
learn_rate = 2.0
weight_decay = 0.1
rms_match = 0.2
clip_limit = 100.0
norm_eps = 1e-06

MESH = pl.DeviceIdType.MESH
BF = jnp.bfloat16
F32 = jnp.float32

CHUNKS = (256, 384, 256)
Q_CUTS = ((0, 256), (256, 640))
Q_PAD = 640


def nt(a, b):
    return lax.dot_general(a, b, (((1,), (1,)), ((), ())), preferred_element_type=F32)


def nn(a, b):
    return lax.dot_general(a, b, (((1,), (0,)), ((), ())), preferred_element_type=F32)


def tn(a, b):
    return lax.dot_general(a, b, (((0,), (0,)), ((), ())), preferred_element_type=F32)


def one_hot(mask):
    return jnp.where(mask, 1.0, 0.0).astype(BF)


def kernel(
    slot_ref, logit_ref, gq_ref, gkv_ref, mq_ref, mkv_ref, wq_ref, wkv_ref,
    wq_out, wkv_out, mq_out, mkv_out,
    xq, xkv, qs, place, swap,
    fsa0, fsa1, fsa2, fra0, fra1, fra2, fsb0, fsb1, fsb2, frb0, frb1, frb2,
    bsa0, bsa1, bsa2, bra0, bra1, bra2, bsb0, bsb1, bsb2, brb0, brb1, brb2,
    mbq, mpq, mbkv, mpkv, xt, xk, xf,
    lz, lm, ly, lc, lp,
    core_send, core_recv, log_send, log_recv, fa_send, fa_recv, fb_send, fb_recv,
    ba_send, ba_recv, bb_send, bb_recv,
):
    fsa, fra, fsb, frb = (fsa0, fsa1, fsa2), (fra0, fra1, fra2), (fsb0, fsb1, fsb2), (frb0, frb1, frb2)
    bsa, bra, bsb, brb = (bsa0, bsa1, bsa2), (bra0, bra1, bra2), (bsb0, bsb1, bsb2), (brb0, brb1, brb2)
    me = lax.axis_index("dp")
    core = lax.axis_index("ctx")
    other = 1 - core
    z = lax.rem(me, GZ)
    yx = lax.div(me, GZ)
    y = lax.div(yx, GX)
    x = lax.rem(yx, GX)
    total = GZ * GYX
    heads = slot_ref.shape[1]
    qw = mq_ref.shape[0]

    def z_peer(i):
        step = i // 2 + 1
        sign = 1 - 2 * (i % 2)
        return lax.rem(z + sign * step + GZ, GZ)

    def yx_peer(i):
        j = i + 1
        return lax.rem(y + j // GX, GY) * GX + lax.rem(x + j % GX, GX)

    def z_dev(zt):
        return (yx * GZ + zt, core)

    def yx_dev(yxt):
        return (yxt * GZ + z, core)

    barrier = pltpu.get_barrier_semaphore()

    def greet_z(i, carry):
        pl.semaphore_signal(barrier, inc=1, device_id=z_dev(z_peer(i)), device_id_type=MESH)
        return carry

    def greet_yx(i, carry):
        pl.semaphore_signal(barrier, inc=1, device_id=yx_dev(yx_peer(i)), device_id_type=MESH)
        return carry

    pl.semaphore_signal(barrier, inc=1, device_id=(me, other), device_id_type=MESH)
    lax.fori_loop(0, GZ - 1, greet_z, 0)
    lax.fori_loop(0, GYX - 1, greet_yx, 0)

    rows = lax.broadcasted_iota(jnp.int32, (total, heads), 0)
    place[...] = one_hot(slot_ref[...] == (rows % GYX) * GZ + rows // GYX)
    rows = lax.broadcasted_iota(jnp.int32, (total, total), 0)
    cols = lax.broadcasted_iota(jnp.int32, (total, total), 1)
    swap[...] = one_hot(cols == (rows % GZ) * GYX + rows // GZ)
    qs[qw:, :] = jnp.zeros((Q_PAD - qw, heads), BF)
    xf[qw:, :] = jnp.zeros((Q_PAD - qw, total), BF)

    pl.semaphore_wait(barrier, GZ - 1 + GYX - 1 + 1)

    def to_core(src, dst, slot):
        return pltpu.make_async_remote_copy(
            src_ref=src, dst_ref=dst, send_sem=core_send.at[slot], recv_sem=core_recv.at[slot],
            device_id=(me, other), device_id_type=MESH,
        )

    core_q = to_core(gq_ref.at[other], xq, 0)
    core_kv = to_core(gkv_ref.at[other], xkv, 1)
    core_q.start()
    core_kv.start()

    def all_z(src, dst, send_sem, recv_sem):
        def body(i, carry):
            zt = z_peer(i)
            pltpu.make_async_remote_copy(
                src_ref=src.at[pl.ds(pl.multiple_of(zt * GYX, GYX), GYX)],
                dst_ref=dst.at[pl.ds(pl.multiple_of(z * GYX, GYX), GYX)],
                send_sem=send_sem, recv_sem=recv_sem,
                device_id=z_dev(zt), device_id_type=MESH,
            ).start()
            return carry

        lax.fori_loop(0, GZ - 1, body, 0)
        mine = pl.ds(pl.multiple_of(z * GYX, GYX), GYX)
        dst[mine, :] = src[mine, :]

    def all_yx(src, dst, send_sem, recv_sem):
        def body(i, carry):
            yxt = yx_peer(i)
            pltpu.make_async_remote_copy(
                src_ref=src.at[pl.ds(pl.multiple_of(yxt * GZ, GZ), GZ)],
                dst_ref=dst.at[pl.ds(pl.multiple_of(yx * GZ, GZ), GZ)],
                send_sem=send_sem, recv_sem=recv_sem,
                device_id=yx_dev(yxt), device_id_type=MESH,
            ).start()
            return carry

        lax.fori_loop(0, GYX - 1, body, 0)
        mine = pl.ds(pl.multiple_of(yx * GZ, GZ), GZ)
        dst[mine, :] = src[mine, :]

    def wait_rows(buf, count, sem):
        view = buf.at[pl.ds(0, count)]
        pltpu.make_async_copy(view, view, sem).wait()

    def wait_z(buf, sem):
        wait_rows(buf, (GZ - 1) * GYX, sem)

    def wait_yx(buf, sem):
        wait_rows(buf, (GYX - 1) * GZ, sem)

    def logits_z(i, carry):
        pltpu.make_async_remote_copy(
            src_ref=logit_ref, dst_ref=lz.at[z], send_sem=log_send.at[0], recv_sem=log_recv.at[0],
            device_id=z_dev(z_peer(i)), device_id_type=MESH,
        ).start()
        return carry

    def logits_yx(i, carry):
        pltpu.make_async_remote_copy(
            src_ref=lm, dst_ref=ly.at[yx], send_sem=log_send.at[1], recv_sem=log_recv.at[1],
            device_id=yx_dev(yx_peer(i)), device_id_type=MESH,
        ).start()
        return carry

    lax.fori_loop(0, GZ - 1, logits_z, 0)
    lz[z] = logit_ref[...]

    core_q.wait()
    qs[:qw, :] = (gq_ref[core].astype(F32) + xq[...].astype(F32)).astype(BF)
    for n, (low, high) in enumerate(Q_CUTS):
        fsa[n][...] = nt(place[...], qs[low:high, :]).astype(BF)
        all_z(fsa[n], fra[n], fa_send.at[n], fa_recv.at[n])
    core_kv.wait()
    kvs = (gkv_ref[core].astype(F32) + xkv[...].astype(F32)).astype(BF)
    fsa[2][...] = nn(place[...], kvs).astype(BF)
    all_z(fsa[2], fra[2], fa_send.at[2], fa_recv.at[2])

    pltpu.make_async_copy(
        lz.at[pl.ds(0, GZ - 1)], lz.at[pl.ds(0, GZ - 1)], log_recv.at[0]
    ).wait()
    lm[...] = jnp.max(lz[...], axis=0)
    lax.fori_loop(0, GYX - 1, logits_yx, 0)
    ly[yx] = lm[...]

    def forward_mid(n):
        wait_z(fra[n], fa_recv.at[n])
        fsb[n][...] = nn(swap[...], fra[n][...]).astype(BF)
        all_yx(fsb[n], frb[n], fb_send.at[n], fb_recv.at[n])

    forward_mid(0)
    forward_mid(1)

    squares = jnp.zeros((1, 1), F32)
    for n, (low, high) in enumerate(Q_CUTS):
        wait_yx(frb[n], fb_recv.at[n])
        real = min(high, qw) - low
        size = high - low
        eye = one_hot(
            lax.broadcasted_iota(jnp.int32, (real, size), 0) == lax.broadcasted_iota(jnp.int32, (real, size), 1)
        )
        fresh = momentum_rate * mq_ref[low : low + real, :] + nt(eye, frb[n][...])
        mq_out[low : low + real, :] = fresh
        mbq[low : low + real, :] = fresh.astype(BF)
        squares = squares + jnp.sum(fresh * fresh, keepdims=True)
    core_mq = to_core(mbq, mpq, 2)
    core_mq.start()
    core_mq.wait()
    theirs = mpq[...].astype(F32)
    squares = squares + jnp.sum(theirs * theirs, keepdims=True)
    scale = 1.0 / (jnp.sqrt(squares) + norm_eps)
    parts = qw // QDIM
    for j in range(parts):
        band = slice(j * QDIM, (j + 1) * QDIM)
        xt[:, j * total : (j + 1) * total] = (mq_out[band, :] * scale).astype(BF)
        lane = (parts + j) * total
        xt[:, lane : lane + total] = (mpq[band, :].astype(F32) * scale).astype(BF)

    def newton(ref, width):
        gram = nt(ref[...], ref[...]).astype(BF)
        mixer = (newton_b * gram.astype(F32) + newton_c * nn(gram, gram)).astype(BF)
        for low in range(0, width, total):
            piece = ref[:, low : low + total]
            yield low, (newton_a * piece.astype(F32) + nn(mixer, piece)).astype(BF)

    for iteration in range(ITERS - 1):
        for low, piece in newton(xt, 2 * parts * total):
            xt[:, low : low + total] = piece
    for low, piece in newton(xt, parts * total):
        j = low // total
        xf[j * QDIM : (j + 1) * QDIM, :] = piece

    for n, (low, high) in enumerate(Q_CUTS):
        bsa[n][...] = nt(swap[...], xf[low:high, :]).astype(BF)
        all_z(bsa[n], bra[n], ba_send.at[n], ba_recv.at[n])

    forward_mid(2)
    wait_yx(frb[2], fb_recv.at[2])
    fresh = momentum_rate * mkv_ref[...] + frb[2][...].astype(F32)
    mkv_out[...] = fresh
    mbkv[...] = fresh.astype(BF)
    core_mkv = to_core(mbkv, mpkv, 3)
    core_mkv.start()
    squares = jnp.sum(fresh * fresh, keepdims=True)
    core_mkv.wait()
    theirs = mpkv[...].astype(F32)
    squares = squares + jnp.sum(theirs * theirs, keepdims=True)
    scale = 1.0 / (jnp.sqrt(squares) + norm_eps)
    eye = one_hot(
        lax.broadcasted_iota(jnp.int32, (KVDIM, KVDIM), 0) == lax.broadcasted_iota(jnp.int32, (KVDIM, KVDIM), 1)
    )
    xk[:, :total] = nt(eye, (mkv_out[...] * scale).astype(BF)).astype(BF)
    xk[:, total:] = nt(eye, (theirs * scale).astype(BF)).astype(BF)
    for iteration in range(ITERS - 1):
        for low, piece in newton(xk, 2 * total):
            xk[:, low : low + total] = piece
    for low, piece in newton(xk, total):
        bsa[2][...] = nt(swap[...], piece).astype(BF)
    all_z(bsa[2], bra[2], ba_send.at[2], ba_recv.at[2])

    def back_mid(n):
        wait_z(bra[n], ba_recv.at[n])
        bsb[n][...] = nn(swap[...], bra[n][...]).astype(BF)
        all_yx(bsb[n], brb[n], bb_send.at[n], bb_recv.at[n])

    back_mid(0)
    back_mid(1)

    pltpu.make_async_copy(
        ly.at[pl.ds(0, GYX - 1)], ly.at[pl.ds(0, GYX - 1)], log_recv.at[1]
    ).wait()
    lc[...] = jnp.max(ly[...], axis=0)
    core_peak = to_core(lc, lp, 4)
    core_peak.start()
    core_peak.wait()
    peak = jnp.maximum(lc[...], lp[...])
    clip = jnp.minimum(1.0, clip_limit / peak)
    root = jnp.sqrt(clip)

    back_mid(2)

    pick = one_hot(slot_ref[...] == lax.broadcasted_iota(jnp.int32, (total, heads), 0))
    scale = rms_match * math.sqrt(max(QRANK, QDIM))
    for n, (low, high) in enumerate(Q_CUTS):
        wait_yx(brb[n], bb_recv.at[n])
        real = min(high, qw) - low
        size = high - low
        update = tn(brb[n][...], pick)[:real, :]
        wide = wq_ref[low : low + real, :].astype(F32)
        fresh = wide - learn_rate * (scale * update + weight_decay * wide)
        column = (lax.broadcasted_iota(jnp.int32, (real, heads), 0) + low) % QDIM
        factor = jnp.where(column < NOPE, root, clip)
        wq_out[low : low + real, :] = (fresh * factor).astype(BF)

    scale = rms_match * math.sqrt(max(KVRANK, KVDIM))
    wait_yx(brb[2], bb_recv.at[2])
    update = tn(pick, brb[2][...])
    wide = wkv_ref[...].astype(F32)
    fresh = wide - learn_rate * (scale * update + weight_decay * wide)
    root_rows = jnp.transpose(jnp.broadcast_to(root, (NOPE, heads)))
    wkv_out[:, :NOPE] = (fresh[:, :NOPE] * root_rows).astype(BF)
    wkv_out[:, NOPE:] = fresh[:, NOPE:].astype(BF)

    for n in range(3):
        wait_z(fsa[n], fa_send.at[n])
        wait_z(bsa[n], ba_send.at[n])
        wait_yx(fsb[n], fb_send.at[n])
        wait_yx(bsb[n], bb_send.at[n])
    pltpu.make_async_copy(
        lz.at[pl.ds(0, GZ - 1)], lz.at[pl.ds(0, GZ - 1)], log_send.at[0]
    ).wait()
    pltpu.make_async_copy(
        ly.at[pl.ds(0, GYX - 1)], ly.at[pl.ds(0, GYX - 1)], log_send.at[1]
    ).wait()


def local(q_weight, kv_weight, q_grad, kv_grad, q_moment, kv_moment, logit_part, slot_table):
    heads = q_weight.shape[0]
    total = q_moment.shape[0]
    qw = q_weight.shape[3]
    kvw = kv_weight.shape[3]
    args = (
        slot_table.reshape(1, heads),
        logit_part.reshape(1, heads),
        jnp.transpose(q_grad.reshape(heads, 2, qw), (1, 2, 0)),
        jnp.transpose(kv_grad.reshape(heads, 2, kvw), (1, 0, 2)),
        jnp.transpose(q_moment.reshape(total, qw)),
        kv_moment.reshape(total, kvw),
        jnp.transpose(q_weight.reshape(heads, qw)),
        kv_weight.reshape(heads, kvw),
    )
    out_shape = (
        jax.ShapeDtypeStruct((qw, heads), BF),
        jax.ShapeDtypeStruct((heads, kvw), BF),
        jax.ShapeDtypeStruct((qw, total), F32),
        jax.ShapeDtypeStruct((total, kvw), F32),
    )
    travel = [pltpu.VMEM((total, width), BF) for _ in range(8) for width in CHUNKS]
    parts = qw // QDIM
    vmem = pl.BlockSpec(memory_space=pltpu.VMEM)
    wq, wkv, mq, mkv = pl.pallas_call(
        kernel,
        out_shape=out_shape,
        in_specs=[vmem] * len(args),
        out_specs=tuple([vmem] * 4),
        scratch_shapes=[
            pltpu.VMEM((qw, heads), BF),
            pltpu.VMEM((heads, kvw), BF),
            pltpu.VMEM((Q_PAD, heads), BF),
            pltpu.VMEM((total, heads), BF),
            pltpu.VMEM((total, total), BF),
            *travel,
            pltpu.VMEM((qw, total), BF),
            pltpu.VMEM((qw, total), BF),
            pltpu.VMEM((total, kvw), BF),
            pltpu.VMEM((total, kvw), BF),
            pltpu.VMEM((QDIM, 2 * parts * total), BF),
            pltpu.VMEM((KVDIM, 2 * total), BF),
            pltpu.VMEM((Q_PAD, total), BF),
            pltpu.VMEM((GZ, 1, heads), F32),
            pltpu.VMEM((1, heads), F32),
            pltpu.VMEM((GYX, 1, heads), F32),
            pltpu.VMEM((1, heads), F32),
            pltpu.VMEM((1, heads), F32),
            pltpu.SemaphoreType.DMA((5,)),
            pltpu.SemaphoreType.DMA((5,)),
            pltpu.SemaphoreType.DMA((2,)),
            pltpu.SemaphoreType.DMA((2,)),
            *[pltpu.SemaphoreType.DMA((3,)) for _ in range(8)],
        ],
        compiler_params=pltpu.CompilerParams(
            collective_id=0, has_side_effects=True, vmem_limit_bytes=48 * 1024 * 1024
        ),
        cost_estimate=pl.CostEstimate(flops=4_000_000_000, bytes_accessed=4_000_000, transcendentals=0),
    )(*args)
    return (
        jnp.transpose(wq).reshape(q_weight.shape),
        wkv.reshape(kv_weight.shape),
        jnp.transpose(mq).reshape(q_moment.shape),
        mkv.reshape(kv_moment.shape),
    )


def solution(mesh):
    in_specs = (
        P(None, "dp", "ctx", None),
        P(None, "dp", "ctx", None),
        P("ctx", None, "dp", None, None),
        P("ctx", None, "dp", None, None),
        P(None, "ctx", "dp", None),
        P(None, "ctx", "dp", None),
        P("dp", "ctx", None),
        P(),
    )
    out_specs = (
        P(None, "dp", "ctx", None),
        P(None, "dp", "ctx", None),
        P(None, "ctx", "dp", None),
        P(None, "ctx", "dp", None),
    )
    return jax.shard_map(local, mesh=mesh, in_specs=in_specs, out_specs=out_specs, check_vma=False)
```

```python
import math

import jax
import jax.numpy as jnp
from jax import lax
from jax.experimental import pallas as pl
from jax.experimental.pallas import tpu as pltpu
from jax.sharding import PartitionSpec as P

NOPE = 128
ITERS = 5
QDIM = 192
KVDIM = 256

GY = 4
GX = 4
GZ = 16
GYX = GY * GX
QRANK = 1536
KVRANK = 512

newton_a = 3.4445
newton_b = -4.775
newton_c = 2.0315
momentum_rate = 0.95
learn_rate = 2.0
weight_decay = 0.1
rms_match = 0.2
clip_limit = 100.0
norm_eps = 1e-06

MESH = pl.DeviceIdType.MESH
BF = jnp.bfloat16
F32 = jnp.float32

CHUNKS = (256, 384, 256)
Q_CUTS = ((0, 256), (256, 640))
Q_PAD = 640
VMEM_LIMIT = 62 * 1024 * 1024


def nt(a, b):
    return lax.dot_general(a, b, (((1,), (1,)), ((), ())), preferred_element_type=F32)


def nn(a, b):
    return lax.dot_general(a, b, (((1,), (0,)), ((), ())), preferred_element_type=F32)


def tn(a, b):
    return lax.dot_general(a, b, (((0,), (0,)), ((), ())), preferred_element_type=F32)


def one_hot(mask):
    return jnp.where(mask, 1.0, 0.0).astype(BF)


def kernel(
    slot_hbm, logit_hbm, gq_hbm, gkv_hbm, mq_hbm, mkv_hbm,
    uq_hbm, ukv_hbm, mq_new_hbm, mkv_new_hbm, peak_hbm,
    slot_ref, logit_ref, gq_ref, gkv_ref, mq_ref, mkv_ref,
    uq_out, ukv_out, mq_out, mkv_out, peak_out,
    xq, xkv, okv, skv, qs, place, swap,
    fsa0, fsa1, fsa2, fra0, fra1, fra2, fsb0, fsb1, fsb2, frb0, frb1, frb2,
    bsa0, bsa1, bsa2, bra0, bra1, bra2, bsb0, bsb1, bsb2, brb0, brb1, brb2,
    mbq, mpq, mbkv, mpkv, xt, xk, xf,
    lz, lm, ly, lc, lp,
    load_sem, store_sem, core_send, core_recv, log_send, log_recv, fa_send, fa_recv, fb_send, fb_recv,
    ba_send, ba_recv, bb_send, bb_recv,
):
    fsa, fra, fsb, frb = (fsa0, fsa1, fsa2), (fra0, fra1, fra2), (fsb0, fsb1, fsb2), (frb0, frb1, frb2)
    bsa, bra, bsb, brb = (bsa0, bsa1, bsa2), (bra0, bra1, bra2), (bsb0, bsb1, bsb2), (brb0, brb1, brb2)
    me = lax.axis_index("dp")
    core = lax.axis_index("ctx")
    other = 1 - core
    z = lax.rem(me, GZ)
    yx = lax.div(me, GZ)
    y = lax.div(yx, GX)
    x = lax.rem(yx, GX)
    total = GZ * GYX
    heads = slot_ref.shape[1]
    qw = mq_ref.shape[0]
    lanes = mkv_ref.shape[1]
    halves = KVDIM // lanes

    def z_peer(i):
        j = i + 1
        step = GZ // 2 - j // 2
        sign = 1 - 2 * (j % 2)
        return lax.rem(z + sign * step + GZ, GZ)

    def yx_peer(i):
        j = GYX - 1 - i
        return lax.rem(y + j // GX, GY) * GX + lax.rem(x + j % GX, GX)

    def z_dev(zt):
        return (yx * GZ + zt, core)

    def yx_dev(yxt):
        return (yxt * GZ + z, core)

    barrier = pltpu.get_barrier_semaphore()

    def greet_z(i, carry):
        pl.semaphore_signal(barrier, inc=1, device_id=z_dev(z_peer(i)), device_id_type=MESH)
        return carry

    def greet_yx(i, carry):
        pl.semaphore_signal(barrier, inc=1, device_id=yx_dev(yx_peer(i)), device_id_type=MESH)
        return carry

    lax.fori_loop(0, GZ - 1, greet_z, 0)
    lax.fori_loop(0, GYX - 1, greet_yx, 0)
    pl.semaphore_signal(barrier, inc=1, device_id=(me, other), device_id_type=MESH)

    loads = [
        pltpu.make_async_copy(src, dst, load_sem.at[n])
        for n, (src, dst) in enumerate(
            (
                (gq_hbm, gq_ref), (gkv_hbm, gkv_ref), (mq_hbm, mq_ref), (mkv_hbm, mkv_ref),
                (slot_hbm, slot_ref), (logit_hbm, logit_ref),
            )
        )
    ]
    stores = [
        pltpu.make_async_copy(src, dst, store_sem.at[n])
        for n, (src, dst) in enumerate(
            (
                (uq_out, uq_hbm), (ukv_out, ukv_hbm), (mq_out, mq_new_hbm), (mkv_out, mkv_new_hbm),
                (peak_out, peak_hbm),
            )
        )
    ]
    for n in (4, 1, 0, 5, 2, 3):
        loads[n].start()

    loads[4].wait()
    rows = lax.broadcasted_iota(jnp.int32, (total, heads), 0)
    place[...] = one_hot(slot_ref[...] == (rows % GYX) * GZ + rows // GYX)
    rows = lax.broadcasted_iota(jnp.int32, (total, total), 0)
    cols = lax.broadcasted_iota(jnp.int32, (total, total), 1)
    swap[...] = one_hot(cols == (rows % GZ) * GYX + rows // GZ)
    qs[qw:, :] = jnp.zeros((Q_PAD - qw, heads), BF)
    xf[qw:, :] = jnp.zeros((Q_PAD - qw, total), BF)

    loads[1].wait()
    cols = lax.broadcasted_iota(jnp.int32, (heads, 2 * halves * heads), 1)
    rows = lax.broadcasted_iota(jnp.int32, (heads, 2 * halves * heads), 0)
    offset = cols - 2 * halves * rows
    for t in range(halves):
        band = slice(t * lanes, (t + 1) * lanes)
        okv[:, band] = nn(one_hot(offset == 2 * t + other), gkv_ref[...]).astype(BF)
        skv[:, band] = nn(one_hot(offset == 2 * t + core), gkv_ref[...]).astype(BF)
    loads[0].wait()
    loads[5].wait()

    pl.semaphore_wait(barrier, GZ - 1 + GYX - 1 + 1)

    def to_core(src, dst, slot):
        return pltpu.make_async_remote_copy(
            src_ref=src, dst_ref=dst, send_sem=core_send.at[slot], recv_sem=core_recv.at[slot],
            device_id=(me, other), device_id_type=MESH,
        )

    spans = tuple(slice(low, min(high, qw)) for low, high in Q_CUTS)
    core_q = [to_core(gq_ref.at[other, span], xq.at[span], n) for n, span in enumerate(spans)]
    core_kv = to_core(okv, xkv, 2)
    for copy in core_q:
        copy.start()
    core_kv.start()

    def send_z(src, dst, send_sem, recv_sem, zt):
        pltpu.make_async_remote_copy(
            src_ref=src.at[pl.ds(pl.multiple_of(zt * GYX, GYX), GYX)],
            dst_ref=dst.at[pl.ds(pl.multiple_of(z * GYX, GYX), GYX)],
            send_sem=send_sem, recv_sem=recv_sem,
            device_id=z_dev(zt), device_id_type=MESH,
        ).start()

    def keep_z(src, dst):
        mine = pl.ds(pl.multiple_of(z * GYX, GYX), GYX)
        dst[mine, :] = src[mine, :]

    def some_z(n, parity):
        odd = lax.rem(z + parity, 2)

        def body(i, carry):
            j = i + 1 - odd
            step = GZ // 2 - odd - 2 * (j // 2)
            sign = 1 - 2 * (j % 2)
            send_z(fsa[n], fra[n], fa_send.at[n], fa_recv.at[n], lax.rem(z + sign * step + GZ, GZ))
            return carry

        lax.fori_loop(0, GZ // 2 - 1 + odd, body, 0)

    def all_z(src, dst, send_sem, recv_sem):
        def body(i, carry):
            send_z(src, dst, send_sem, recv_sem, z_peer(i))
            return carry

        lax.fori_loop(0, GZ - 1, body, 0)
        keep_z(src, dst)

    def all_yx(src, dst, send_sem, recv_sem):
        def body(i, carry):
            yxt = yx_peer(i)
            pltpu.make_async_remote_copy(
                src_ref=src.at[pl.ds(pl.multiple_of(yxt * GZ, GZ), GZ)],
                dst_ref=dst.at[pl.ds(pl.multiple_of(yx * GZ, GZ), GZ)],
                send_sem=send_sem, recv_sem=recv_sem,
                device_id=yx_dev(yxt), device_id_type=MESH,
            ).start()
            return carry

        lax.fori_loop(0, GYX - 1, body, 0)
        mine = pl.ds(pl.multiple_of(yx * GZ, GZ), GZ)
        dst[mine, :] = src[mine, :]

    def wait_rows(buf, count, sem):
        view = buf.at[pl.ds(0, count)]
        pltpu.make_async_copy(view, view, sem).wait()

    def wait_z(buf, sem):
        wait_rows(buf, (GZ - 1) * GYX, sem)

    def wait_yx(buf, sem):
        wait_rows(buf, (GYX - 1) * GZ, sem)

    def logits_z(i, carry):
        pltpu.make_async_remote_copy(
            src_ref=logit_ref, dst_ref=lz.at[z], send_sem=log_send.at[0], recv_sem=log_recv.at[0],
            device_id=z_dev(z_peer(i)), device_id_type=MESH,
        ).start()
        return carry

    def logits_yx(i, carry):
        pltpu.make_async_remote_copy(
            src_ref=lm, dst_ref=ly.at[yx], send_sem=log_send.at[1], recv_sem=log_recv.at[1],
            device_id=yx_dev(yx_peer(i)), device_id_type=MESH,
        ).start()
        return carry

    lax.fori_loop(0, GZ - 1, logits_z, 0)
    lz[z] = logit_ref[...]

    for n, (low, high) in enumerate(Q_CUTS):
        core_q[n].wait()
        span = spans[n]
        qs[span, :] = (gq_ref[core, span].astype(F32) + xq[span, :].astype(F32)).astype(BF)
        fsa[n][...] = nt(place[...], qs[low:high, :]).astype(BF)
        some_z(n, 0)
    for n in range(2):
        some_z(n, 1)
        keep_z(fsa[n], fra[n])
    core_kv.wait()
    kvs = (skv[...].astype(F32) + xkv[...].astype(F32)).astype(BF)
    fsa[2][...] = nn(place[...], kvs).astype(BF)
    some_z(2, 0)
    some_z(2, 1)
    keep_z(fsa[2], fra[2])

    def forward_mid(n):
        wait_z(fra[n], fa_recv.at[n])
        fsb[n][...] = nn(swap[...], fra[n][...]).astype(BF)
        all_yx(fsb[n], frb[n], fb_send.at[n], fb_recv.at[n])

    loads[2].wait()
    loads[3].wait()
    forward_mid(0)
    forward_mid(1)
    forward_mid(2)

    view = lz.at[pl.ds(0, GZ - 1)]
    pltpu.make_async_copy(view, view, log_recv.at[0]).wait()
    lm[...] = jnp.max(lz[...], axis=0)
    lax.fori_loop(0, GYX - 1, logits_yx, 0)
    ly[yx] = lm[...]

    squares = jnp.zeros((1, 1), F32)
    core_mq = [to_core(mbq.at[span], mpq.at[span], 3 + n) for n, span in enumerate(spans)]
    for n, (low, high) in enumerate(Q_CUTS):
        wait_yx(frb[n], fb_recv.at[n])
        span = spans[n]
        real = min(high, qw) - low
        size = high - low
        eye = one_hot(
            lax.broadcasted_iota(jnp.int32, (real, size), 0) == lax.broadcasted_iota(jnp.int32, (real, size), 1)
        )
        fresh = momentum_rate * mq_ref[span, :] + nt(eye, frb[n][...])
        mq_out[span, :] = fresh
        mbq[span, :] = fresh.astype(BF)
        core_mq[n].start()
        squares = squares + jnp.sum(fresh * fresh, keepdims=True)
    for n, span in enumerate(spans):
        core_mq[n].wait()
        theirs = mpq[span, :].astype(F32)
        squares = squares + jnp.sum(theirs * theirs, keepdims=True)
    stores[2].start()
    scale = 1.0 / (jnp.sqrt(squares) + norm_eps)
    parts = qw // QDIM
    for j in range(parts):
        band = slice(j * QDIM, (j + 1) * QDIM)
        xt[:, j * total : (j + 1) * total] = (mq_out[band, :] * scale).astype(BF)
        lane = (parts + j) * total
        xt[:, lane : lane + total] = (mpq[band, :].astype(F32) * scale).astype(BF)

    def newton(ref, width):
        gram = nt(ref[...], ref[...]).astype(BF)
        mixer = (newton_b * gram.astype(F32) + newton_c * nn(gram, gram)).astype(BF)
        for low in range(0, width, total):
            piece = ref[:, low : low + total]
            yield low, (newton_a * piece.astype(F32) + nn(mixer, piece)).astype(BF)

    for iteration in range(ITERS - 1):
        for low, piece in newton(xt, 2 * parts * total):
            xt[:, low : low + total] = piece
    for low, piece in newton(xt, parts * total):
        j = low // total
        xf[j * QDIM : (j + 1) * QDIM, :] = piece

    for n, (low, high) in enumerate(Q_CUTS):
        bsa[n][...] = nt(swap[...], xf[low:high, :]).astype(BF)
        all_z(bsa[n], bra[n], ba_send.at[n], ba_recv.at[n])

    wait_yx(frb[2], fb_recv.at[2])
    for t in range(halves):
        band = slice(t * lanes, (t + 1) * lanes)
        picked = pl.ds(t, total, stride=halves)
        fresh = momentum_rate * mkv_ref[picked, :] + frb[2][:, band].astype(F32)
        mkv_out[picked, :] = fresh
        mbkv[:, band] = fresh.astype(BF)
    core_mkv = to_core(mbkv, mpkv, 5)
    core_mkv.start()
    stores[3].start()
    ours = mkv_out[...]
    squares = jnp.sum(ours * ours, keepdims=True)
    eye = one_hot(
        lax.broadcasted_iota(jnp.int32, (lanes, lanes), 0) == lax.broadcasted_iota(jnp.int32, (lanes, lanes), 1)
    )
    core_mkv.wait()
    theirs = mpkv[...].astype(F32)
    squares = squares + jnp.sum(theirs * theirs, keepdims=True)
    scale = 1.0 / (jnp.sqrt(squares) + norm_eps)
    for t in range(halves):
        band = slice(t * lanes, (t + 1) * lanes)
        ours = mkv_out[pl.ds(t, total, stride=halves), :]
        xk[band, :total] = nt(eye, (ours * scale).astype(BF)).astype(BF)
        xk[band, total:] = nt(eye, (theirs[:, band] * scale).astype(BF)).astype(BF)
    for iteration in range(ITERS - 1):
        for low, piece in newton(xk, 2 * total):
            xk[:, low : low + total] = piece
    for low, piece in newton(xk, total):
        bsa[2][...] = nt(swap[...], piece).astype(BF)
    all_z(bsa[2], bra[2], ba_send.at[2], ba_recv.at[2])

    view = ly.at[pl.ds(0, GYX - 1)]
    pltpu.make_async_copy(view, view, log_recv.at[1]).wait()
    lc[...] = jnp.max(ly[...], axis=0)
    core_peak = to_core(lc, lp, 6)
    core_peak.start()
    core_peak.wait()
    peak_out[...] = jnp.maximum(lc[...], lp[...])
    stores[4].start()

    def back_mid(n):
        wait_z(bra[n], ba_recv.at[n])
        bsb[n][...] = nn(swap[...], bra[n][...]).astype(BF)
        all_yx(bsb[n], brb[n], bb_send.at[n], bb_recv.at[n])

    back_mid(0)
    back_mid(1)
    back_mid(2)

    pick = one_hot(slot_ref[...] == lax.broadcasted_iota(jnp.int32, (total, heads), 0))
    for n, (low, high) in enumerate(Q_CUTS):
        wait_yx(brb[n], bb_recv.at[n])
        real = min(high, qw) - low
        uq_out[spans[n], :] = tn(brb[n][...], pick)[:real, :].astype(BF)
    stores[0].start()
    for n in range(3):
        wait_z(fsa[n], fa_send.at[n])
        wait_z(bsa[n], ba_send.at[n])
        wait_yx(fsb[n], fb_send.at[n])
    view = lz.at[pl.ds(0, GZ - 1)]
    pltpu.make_async_copy(view, view, log_send.at[0]).wait()
    view = ly.at[pl.ds(0, GYX - 1)]
    pltpu.make_async_copy(view, view, log_send.at[1]).wait()
    wait_yx(brb[2], bb_recv.at[2])
    ukv_out[...] = tn(pick, brb[2][...]).astype(BF)
    stores[1].start()
    for n in range(3):
        wait_yx(bsb[n], bb_send.at[n])
    for store in stores:
        store.wait()


def finish(
    peak_hbm, uq_hbm, ukv_hbm, wq_hbm, wkv_hbm, mq_hbm, mkv_hbm,
    wq_out, wkv_out, mq_out, mkv_out,
    mq_ref, mkv_ref, peak_ref, uq_ref, ukv_ref, wq_ref, wkv_ref, new_q, new_kv, load_sem, sem,
):
    loads = [
        pltpu.make_async_copy(src, dst, load_sem.at[n])
        for n, (src, dst) in enumerate(
            (
                (peak_hbm, peak_ref), (uq_hbm, uq_ref), (wq_hbm, wq_ref), (ukv_hbm, ukv_ref), (wkv_hbm, wkv_ref),
                (mq_hbm, mq_ref), (mkv_hbm, mkv_ref),
            )
        )
    ]
    for load in loads:
        load.start()
    copies = [
        pltpu.make_async_copy(src, dst, sem.at[n])
        for n, (src, dst) in enumerate(
            ((mq_ref, mq_out), (mkv_ref, mkv_out), (new_q, wq_out), (new_kv, wkv_out))
        )
    ]
    qw, heads = wq_ref.shape
    for load in loads[:3]:
        load.wait()
    clip = jnp.minimum(1.0, clip_limit / peak_ref[...])
    root = jnp.sqrt(clip)
    scale = rms_match * math.sqrt(max(QRANK, QDIM))
    for low in range(0, qw, QDIM):
        for start, stop, factor in ((low, low + NOPE, root), (low + NOPE, low + QDIM, clip)):
            wide = wq_ref[start:stop, :].astype(F32)
            fresh = wide - learn_rate * (scale * uq_ref[start:stop, :].astype(F32) + weight_decay * wide)
            new_q[start:stop, :] = (fresh * factor).astype(BF)
    copies[2].start()
    for load in loads[5:]:
        load.wait()
    copies[0].start()
    copies[1].start()
    for load in loads[3:5]:
        load.wait()
    scale = rms_match * math.sqrt(max(KVRANK, KVDIM))
    wide = wkv_ref[...].astype(F32)
    fresh = wide - learn_rate * (scale * ukv_ref[...].astype(F32) + weight_decay * wide)
    root_rows = jnp.transpose(jnp.broadcast_to(root, (NOPE, heads)))
    new_kv[:, :NOPE] = (fresh[:, :NOPE] * root_rows).astype(BF)
    new_kv[:, NOPE:] = fresh[:, NOPE:].astype(BF)
    copies[3].start()
    for copy in copies:
        copy.wait()


def local(q_weight, kv_weight, q_grad, kv_grad, q_moment, kv_moment, logit_part, slot_table):
    heads = q_weight.shape[0]
    total = q_moment.shape[0]
    qw = q_weight.shape[3]
    kvw = kv_weight.shape[3]
    lanes = 128
    halves = kvw // lanes
    parts = qw // QDIM
    hbm = pl.BlockSpec(memory_space=pl.ANY)
    split = kv_grad.reshape(heads, 2, halves, lanes)
    travel = [pltpu.VMEM((total, width), BF) for _ in range(8) for width in CHUNKS]
    uq, ukv, mq, mkv, peak = pl.pallas_call(
        kernel,
        out_shape=(
            jax.ShapeDtypeStruct((qw, heads), BF),
            jax.ShapeDtypeStruct((heads, kvw), BF),
            jax.ShapeDtypeStruct((qw, total), F32),
            jax.ShapeDtypeStruct((halves * total, lanes), F32),
            jax.ShapeDtypeStruct((1, heads), F32),
        ),
        in_specs=[hbm] * 6,
        out_specs=tuple([hbm] * 5),
        scratch_shapes=[
            pltpu.VMEM((1, heads), jnp.int32),
            pltpu.VMEM((1, heads), F32),
            pltpu.VMEM((2, qw, heads), BF),
            pltpu.VMEM((2 * halves * heads, lanes), BF),
            pltpu.VMEM((qw, total), F32),
            pltpu.VMEM((halves * total, lanes), F32),
            pltpu.VMEM((qw, heads), BF),
            pltpu.VMEM((heads, kvw), BF),
            pltpu.VMEM((qw, total), F32),
            pltpu.VMEM((halves * total, lanes), F32),
            pltpu.VMEM((1, heads), F32),
            pltpu.VMEM((qw, heads), BF),
            pltpu.VMEM((heads, kvw), BF),
            pltpu.VMEM((heads, kvw), BF),
            pltpu.VMEM((heads, kvw), BF),
            pltpu.VMEM((Q_PAD, heads), BF),
            pltpu.VMEM((total, heads), BF),
            pltpu.VMEM((total, total), BF),
            *travel,
            pltpu.VMEM((qw, total), BF),
            pltpu.VMEM((qw, total), BF),
            pltpu.VMEM((total, kvw), BF),
            pltpu.VMEM((total, kvw), BF),
            pltpu.VMEM((QDIM, 2 * parts * total), BF),
            pltpu.VMEM((KVDIM, 2 * total), BF),
            pltpu.VMEM((Q_PAD, total), BF),
            pltpu.VMEM((GZ, 1, heads), F32),
            pltpu.VMEM((1, heads), F32),
            pltpu.VMEM((GYX, 1, heads), F32),
            pltpu.VMEM((1, heads), F32),
            pltpu.VMEM((1, heads), F32),
            pltpu.SemaphoreType.DMA((6,)),
            pltpu.SemaphoreType.DMA((5,)),
            pltpu.SemaphoreType.DMA((7,)),
            pltpu.SemaphoreType.DMA((7,)),
            pltpu.SemaphoreType.DMA((2,)),
            pltpu.SemaphoreType.DMA((2,)),
            *[pltpu.SemaphoreType.DMA((3,)) for _ in range(8)],
        ],
        compiler_params=pltpu.CompilerParams(
            collective_id=0, has_side_effects=True, vmem_limit_bytes=VMEM_LIMIT
        ),
        cost_estimate=pl.CostEstimate(flops=4_000_000_000, bytes_accessed=4_000_000, transcendentals=0),
    )(
        slot_table.reshape(1, heads),
        logit_part.reshape(1, heads),
        jnp.transpose(q_grad.reshape(heads, 2, qw), (1, 2, 0)),
        jnp.transpose(split, (0, 2, 1, 3)).reshape(2 * halves * heads, lanes),
        jnp.transpose(q_moment.reshape(total, qw)),
        kv_moment.reshape(halves * total, lanes),
    )
    wq, wkv, mq, mkv = pl.pallas_call(
        finish,
        out_shape=(
            jax.ShapeDtypeStruct((qw, heads), BF),
            jax.ShapeDtypeStruct((heads, kvw), BF),
            jax.ShapeDtypeStruct((qw, total), F32),
            jax.ShapeDtypeStruct((halves * total, lanes), F32),
        ),
        in_specs=[hbm] * 7,
        out_specs=tuple([hbm] * 4),
        scratch_shapes=[
            pltpu.VMEM((qw, total), F32),
            pltpu.VMEM((halves * total, lanes), F32),
            pltpu.VMEM((1, heads), F32),
            pltpu.VMEM((qw, heads), BF),
            pltpu.VMEM((heads, kvw), BF),
            pltpu.VMEM((qw, heads), BF),
            pltpu.VMEM((heads, kvw), BF),
            pltpu.VMEM((qw, heads), BF),
            pltpu.VMEM((heads, kvw), BF),
            pltpu.SemaphoreType.DMA((7,)),
            pltpu.SemaphoreType.DMA((4,)),
        ],
        compiler_params=pltpu.CompilerParams(vmem_limit_bytes=VMEM_LIMIT),
        cost_estimate=pl.CostEstimate(flops=4_000_000, bytes_accessed=4_000_000, transcendentals=0),
    )(peak, uq, ukv, jnp.transpose(q_weight.reshape(heads, qw)), kv_weight.reshape(heads, kvw), mq, mkv)
    return (
        jnp.transpose(wq).reshape(q_weight.shape),
        wkv.reshape(kv_weight.shape),
        jnp.transpose(mq).reshape(q_moment.shape),
        mkv.reshape(kv_moment.shape),
    )


def solution(mesh):
    in_specs = (
        P(None, "dp", "ctx", None),
        P(None, "dp", "ctx", None),
        P("ctx", None, "dp", None, None),
        P("ctx", None, "dp", None, None),
        P(None, "ctx", "dp", None),
        P(None, "ctx", "dp", None),
        P("dp", "ctx", None),
        P(),
    )
    out_specs = (
        P(None, "dp", "ctx", None),
        P(None, "dp", "ctx", None),
        P(None, "ctx", "dp", None),
        P(None, "ctx", "dp", None),
    )
    return jax.shard_map(local, mesh=mesh, in_specs=in_specs, out_specs=out_specs, check_vma=False)
```

```python
import math

import jax
import jax.numpy as jnp
from jax import lax
from jax.experimental import pallas as pl
from jax.experimental.pallas import tpu as pltpu
from jax.sharding import PartitionSpec as P

NOPE = 128
ITERS = 5
QDIM = 192
KVDIM = 256

GY = 4
GX = 4
GZ = 16
GYX = GY * GX
QRANK = 1536
KVRANK = 512

newton_a = 3.4445
newton_b = -4.775
newton_c = 2.0315
momentum_rate = 0.95
learn_rate = 2.0
weight_decay = 0.1
rms_match = 0.2
clip_limit = 100.0
norm_eps = 1e-06

MESH = pl.DeviceIdType.MESH
BF = jnp.bfloat16
F32 = jnp.float32

CHUNKS = (256, 384, 256)
Q_CUTS = ((0, 256), (256, 640))
Q_PAD = 640
Z_FIRST = 1
VMEM_LIMIT = 62 * 1024 * 1024


def nt(a, b):
    return lax.dot_general(a, b, (((1,), (1,)), ((), ())), preferred_element_type=F32)


def nn(a, b):
    return lax.dot_general(a, b, (((1,), (0,)), ((), ())), preferred_element_type=F32)


def tn(a, b):
    return lax.dot_general(a, b, (((0,), (0,)), ((), ())), preferred_element_type=F32)


def one_hot(mask):
    return jnp.where(mask, 1.0, 0.0).astype(BF)


def kernel(
    slot_hbm, logit_hbm, gq_hbm, gkv_hbm, mq_hbm, mkv_hbm,
    uq_hbm, ukv_hbm, mq_new_hbm, mkv_new_hbm, peak_hbm,
    slot_ref, logit_ref, gq_ref, gkv_ref, mq_ref, mkv_ref,
    uq_out, ukv_out, mq_out, mkv_out, peak_out,
    xq, xkv, okv, skv, qs, place, pick, swap,
    fsa0, fsa1, fsa2, fra0, fra1, fra2, fsb0, fsb1, fsb2, frb0, frb1, frb2,
    bsa0, bsa1, bsa2, bra0, bra1, bra2, bsb0, bsb1, bsb2, brb0, brb1, brb2,
    mbq, mpq, mbkv, mpkv, xt, xk, xf,
    lz, lm, ly, lc, lp,
    load_sem, store_sem, core_send, core_recv, log_send, log_recv, fa_send, fa_recv, fb_send, fb_recv,
    ba_send, ba_recv, bb_send, bb_recv,
):
    fsa, fra, fsb, frb = (fsa0, fsa1, fsa2), (fra0, fra1, fra2), (fsb0, fsb1, fsb2), (frb0, frb1, frb2)
    bsa, bra, bsb, brb = (bsa0, bsa1, bsa2), (bra0, bra1, bra2), (bsb0, bsb1, bsb2), (brb0, brb1, brb2)
    me = lax.axis_index("dp")
    core = lax.axis_index("ctx")
    other = 1 - core
    z = lax.rem(me, GZ)
    yx = lax.div(me, GZ)
    y = lax.div(yx, GX)
    x = lax.rem(yx, GX)
    total = GZ * GYX
    heads = slot_ref.shape[1]
    qw = mq_ref.shape[0]
    lanes = mkv_ref.shape[1]
    halves = KVDIM // lanes

    def z_peer(i):
        j = i + 1
        step = GZ // 2 - j // 2
        sign = 1 - 2 * (j % 2)
        return lax.rem(z + sign * step + GZ, GZ)

    def yx_peer(i):
        j = GYX - 1 - i
        return lax.rem(y + j // GX, GY) * GX + lax.rem(x + j % GX, GX)

    def z_dev(zt):
        return (yx * GZ + zt, core)

    def yx_dev(yxt):
        return (yxt * GZ + z, core)

    barrier = pltpu.get_barrier_semaphore()

    def greet_z(i, carry):
        pl.semaphore_signal(barrier, inc=1, device_id=z_dev(z_peer(i)), device_id_type=MESH)
        return carry

    def greet_yx(i, carry):
        pl.semaphore_signal(barrier, inc=1, device_id=yx_dev(yx_peer(i)), device_id_type=MESH)
        return carry

    lax.fori_loop(0, GZ - 1, greet_z, 0)
    lax.fori_loop(0, GYX - 1, greet_yx, 0)
    pl.semaphore_signal(barrier, inc=1, device_id=(me, other), device_id_type=MESH)

    loads = [
        pltpu.make_async_copy(src, dst, load_sem.at[n])
        for n, (src, dst) in enumerate(
            (
                (gq_hbm, gq_ref), (gkv_hbm, gkv_ref), (mq_hbm, mq_ref), (mkv_hbm, mkv_ref),
                (slot_hbm, slot_ref), (logit_hbm, logit_ref),
            )
        )
    ]
    stores = [
        pltpu.make_async_copy(src, dst, store_sem.at[n])
        for n, (src, dst) in enumerate(
            (
                (uq_out, uq_hbm), (ukv_out, ukv_hbm), (mq_out, mq_new_hbm), (mkv_out, mkv_new_hbm),
                (peak_out, peak_hbm),
            )
        )
    ]
    for n in (4, 1, 0, 5, 2, 3):
        loads[n].start()

    loads[4].wait()
    rows = lax.broadcasted_iota(jnp.int32, (total, heads), 0)
    place[...] = one_hot(slot_ref[...] == (rows % GYX) * GZ + rows // GYX)
    pick[...] = one_hot(slot_ref[...] == rows)
    rows = lax.broadcasted_iota(jnp.int32, (total, total), 0)
    cols = lax.broadcasted_iota(jnp.int32, (total, total), 1)
    swap[...] = one_hot(cols == (rows % GZ) * GYX + rows // GZ)
    qs[qw:, :] = jnp.zeros((Q_PAD - qw, heads), BF)
    xf[qw:, :] = jnp.zeros((Q_PAD - qw, total), BF)

    def pick_rows(dst, half):
        cols = lax.broadcasted_iota(jnp.int32, (heads, 2 * halves * heads), 1)
        rows = lax.broadcasted_iota(jnp.int32, (heads, 2 * halves * heads), 0)
        offset = cols - 2 * halves * rows
        for t in range(halves):
            dst[:, t * lanes : (t + 1) * lanes] = nn(one_hot(offset == 2 * t + half), gkv_ref[...]).astype(BF)

    loads[1].wait()
    loads[0].wait()
    loads[5].wait()

    pl.semaphore_wait(barrier, GZ - 1 + GYX - 1 + 1)

    def to_core(src, dst, slot):
        return pltpu.make_async_remote_copy(
            src_ref=src, dst_ref=dst, send_sem=core_send.at[slot], recv_sem=core_recv.at[slot],
            device_id=(me, other), device_id_type=MESH,
        )

    spans = tuple(slice(low, min(high, qw)) for low, high in Q_CUTS)
    core_q = [to_core(gq_ref.at[other, span], xq.at[span], n) for n, span in enumerate(spans)]
    core_kv = to_core(okv, xkv, 2)
    for copy in core_q[::-1]:
        copy.start()
    pick_rows(okv, other)
    core_kv.start()

    def send_z(src, dst, send_sem, recv_sem, zt):
        pltpu.make_async_remote_copy(
            src_ref=src.at[pl.ds(pl.multiple_of(zt * GYX, GYX), GYX)],
            dst_ref=dst.at[pl.ds(pl.multiple_of(z * GYX, GYX), GYX)],
            send_sem=send_sem, recv_sem=recv_sem,
            device_id=z_dev(zt), device_id_type=MESH,
        ).start()

    def keep_z(src, dst):
        mine = pl.ds(pl.multiple_of(z * GYX, GYX), GYX)
        dst[mine, :] = src[mine, :]

    def all_z(src, dst, send_sem, recv_sem):
        def body(i, carry):
            send_z(src, dst, send_sem, recv_sem, z_peer(i))
            return carry

        lax.fori_loop(0, GZ - 1, body, 0)
        keep_z(src, dst)

    def all_yx(src, dst, send_sem, recv_sem):
        def body(i, carry):
            yxt = yx_peer(i)
            pltpu.make_async_remote_copy(
                src_ref=src.at[pl.ds(pl.multiple_of(yxt * GZ, GZ), GZ)],
                dst_ref=dst.at[pl.ds(pl.multiple_of(yx * GZ, GZ), GZ)],
                send_sem=send_sem, recv_sem=recv_sem,
                device_id=yx_dev(yxt), device_id_type=MESH,
            ).start()
            return carry

        lax.fori_loop(0, GYX - 1, body, 0)
        mine = pl.ds(pl.multiple_of(yx * GZ, GZ), GZ)
        dst[mine, :] = src[mine, :]

    def wait_rows(buf, count, sem):
        view = buf.at[pl.ds(0, count)]
        pltpu.make_async_copy(view, view, sem).wait()

    def wait_z(buf, sem):
        wait_rows(buf, (GZ - 1) * GYX, sem)

    def wait_yx(buf, sem):
        wait_rows(buf, (GYX - 1) * GZ, sem)

    def logits_z(i, carry):
        pltpu.make_async_remote_copy(
            src_ref=logit_ref, dst_ref=lz.at[z], send_sem=log_send.at[0], recv_sem=log_recv.at[0],
            device_id=z_dev(z_peer(i)), device_id_type=MESH,
        ).start()
        return carry

    def logits_yx(i, carry):
        pltpu.make_async_remote_copy(
            src_ref=lm, dst_ref=ly.at[yx], send_sem=log_send.at[1], recv_sem=log_recv.at[1],
            device_id=yx_dev(yx_peer(i)), device_id_type=MESH,
        ).start()
        return carry

    lax.fori_loop(0, GZ - 1, logits_z, 0)
    lz[z] = logit_ref[...]

    for n in (1, 0):
        core_q[n].wait()
        low, high = Q_CUTS[n]
        span = spans[n]
        qs[span, :] = (gq_ref[core, span].astype(F32) + xq[span, :].astype(F32)).astype(BF)
        if n == Z_FIRST:
            fsa[n][...] = nt(place[...], qs[low:high, :]).astype(BF)
            all_z(fsa[n], fra[n], fa_send.at[n], fa_recv.at[n])
        else:
            fsa[n][...] = nt(pick[...], qs[low:high, :]).astype(BF)
            all_yx(fsa[n], fra[n], fa_send.at[n], fa_recv.at[n])
    pick_rows(skv, core)
    core_kv.wait()
    kvs = (skv[...].astype(F32) + xkv[...].astype(F32)).astype(BF)
    fsa[2][...] = nn(pick[...], kvs).astype(BF)
    all_yx(fsa[2], fra[2], fa_send.at[2], fa_recv.at[2])

    def second_leg(n, src, mid, dst, first_recv, send_sem, recv_sem):
        wait_rows(src, (GZ - 1) * GYX, first_recv)
        mid[...] = nn(swap[...], src[...]).astype(BF)
        leg = all_yx if n == Z_FIRST else all_z
        leg(mid, dst, send_sem, recv_sem)

    def forward_mid(n):
        second_leg(n, fra[n], fsb[n], frb[n], fa_recv.at[n], fb_send.at[n], fb_recv.at[n])

    loads[2].wait()
    loads[3].wait()
    forward_mid(0)
    forward_mid(2)
    forward_mid(1)

    view = lz.at[pl.ds(0, GZ - 1)]
    pltpu.make_async_copy(view, view, log_recv.at[0]).wait()
    lm[...] = jnp.max(lz[...], axis=0)
    lax.fori_loop(0, GYX - 1, logits_yx, 0)
    ly[yx] = lm[...]

    squares = jnp.zeros((1, 1), F32)
    core_mq = [to_core(mbq.at[span], mpq.at[span], 3 + n) for n, span in enumerate(spans)]
    for n, (low, high) in enumerate(Q_CUTS):
        wait_yx(frb[n], fb_recv.at[n])
        span = spans[n]
        real = min(high, qw) - low
        size = high - low
        if n == Z_FIRST:
            eye = one_hot(
                lax.broadcasted_iota(jnp.int32, (real, size), 0) == lax.broadcasted_iota(jnp.int32, (real, size), 1)
            )
            arrived = nt(eye, frb[n][...])
        else:
            arrived = tn(frb[n][...], swap[...])[:real, :]
        fresh = momentum_rate * mq_ref[span, :] + arrived
        mq_out[span, :] = fresh
        mbq[span, :] = fresh.astype(BF)
        core_mq[n].start()
        squares = squares + jnp.sum(fresh * fresh, keepdims=True)
    for n, span in enumerate(spans):
        core_mq[n].wait()
        theirs = mpq[span, :].astype(F32)
        squares = squares + jnp.sum(theirs * theirs, keepdims=True)
    stores[2].start()
    scale = 1.0 / (jnp.sqrt(squares) + norm_eps)
    parts = qw // QDIM
    for j in range(parts):
        band = slice(j * QDIM, (j + 1) * QDIM)
        xt[:, j * total : (j + 1) * total] = (mq_out[band, :] * scale).astype(BF)
        lane = (parts + j) * total
        xt[:, lane : lane + total] = (mpq[band, :].astype(F32) * scale).astype(BF)

    def newton(ref, width):
        gram = nt(ref[...], ref[...]).astype(BF)
        mixer = (newton_b * gram.astype(F32) + newton_c * nn(gram, gram)).astype(BF)
        for low in range(0, width, total):
            piece = ref[:, low : low + total]
            yield low, (newton_a * piece.astype(F32) + nn(mixer, piece)).astype(BF)

    for iteration in range(ITERS - 1):
        for low, piece in newton(xt, 2 * parts * total):
            xt[:, low : low + total] = piece
    for low, piece in newton(xt, parts * total):
        j = low // total
        xf[j * QDIM : (j + 1) * QDIM, :] = piece

    same = one_hot(
        lax.broadcasted_iota(jnp.int32, (total, total), 0) == lax.broadcasted_iota(jnp.int32, (total, total), 1)
    )
    for n in (1, 0):
        low, high = Q_CUTS[n]
        if n == Z_FIRST:
            bsa[n][...] = nt(swap[...], xf[low:high, :]).astype(BF)
            all_z(bsa[n], bra[n], ba_send.at[n], ba_recv.at[n])
        else:
            bsa[n][...] = nt(same, xf[low:high, :]).astype(BF)
            all_yx(bsa[n], bra[n], ba_send.at[n], ba_recv.at[n])

    wait_yx(frb[2], fb_recv.at[2])
    arrived = nn(swap[...], frb[2][...])
    for t in range(halves):
        band = slice(t * lanes, (t + 1) * lanes)
        picked = pl.ds(t, total, stride=halves)
        fresh = momentum_rate * mkv_ref[picked, :] + arrived[:, band]
        mkv_out[picked, :] = fresh
        mbkv[:, band] = fresh.astype(BF)
    core_mkv = to_core(mbkv, mpkv, 5)
    core_mkv.start()
    stores[3].start()
    ours = mkv_out[...]
    squares = jnp.sum(ours * ours, keepdims=True)
    eye = one_hot(
        lax.broadcasted_iota(jnp.int32, (lanes, lanes), 0) == lax.broadcasted_iota(jnp.int32, (lanes, lanes), 1)
    )
    core_mkv.wait()
    theirs = mpkv[...].astype(F32)
    squares = squares + jnp.sum(theirs * theirs, keepdims=True)
    scale = 1.0 / (jnp.sqrt(squares) + norm_eps)
    for t in range(halves):
        band = slice(t * lanes, (t + 1) * lanes)
        ours = mkv_out[pl.ds(t, total, stride=halves), :]
        xk[band, :total] = nt(eye, (ours * scale).astype(BF)).astype(BF)
        xk[band, total:] = nt(eye, (theirs[:, band] * scale).astype(BF)).astype(BF)
    for iteration in range(ITERS - 1):
        for low, piece in newton(xk, 2 * total):
            xk[:, low : low + total] = piece
    for low, piece in newton(xk, total):
        bsa[2][...] = nt(same, piece).astype(BF)
    all_yx(bsa[2], bra[2], ba_send.at[2], ba_recv.at[2])

    def back_mid(n):
        second_leg(n, bra[n], bsb[n], brb[n], ba_recv.at[n], bb_send.at[n], bb_recv.at[n])

    back_mid(0)

    view = ly.at[pl.ds(0, GYX - 1)]
    pltpu.make_async_copy(view, view, log_recv.at[1]).wait()
    lc[...] = jnp.max(ly[...], axis=0)
    core_peak = to_core(lc, lp, 6)
    core_peak.start()
    core_peak.wait()
    peak_out[...] = jnp.maximum(lc[...], lp[...])
    stores[4].start()

    back_mid(2)
    back_mid(1)

    for n, (low, high) in enumerate(Q_CUTS):
        wait_yx(brb[n], bb_recv.at[n])
        real = min(high, qw) - low
        order = pick if n == Z_FIRST else place
        uq_out[spans[n], :] = tn(brb[n][...], order[...])[:real, :].astype(BF)
    stores[0].start()
    for n in range(3):
        wait_z(fsa[n], fa_send.at[n])
        wait_z(bsa[n], ba_send.at[n])
        wait_yx(fsb[n], fb_send.at[n])
    view = lz.at[pl.ds(0, GZ - 1)]
    pltpu.make_async_copy(view, view, log_send.at[0]).wait()
    view = ly.at[pl.ds(0, GYX - 1)]
    pltpu.make_async_copy(view, view, log_send.at[1]).wait()
    wait_yx(brb[2], bb_recv.at[2])
    ukv_out[...] = tn(place[...], brb[2][...]).astype(BF)
    stores[1].start()
    for n in range(3):
        wait_yx(bsb[n], bb_send.at[n])
    for store in stores:
        store.wait()


def finish(
    peak_hbm, uq_hbm, ukv_hbm, wq_hbm, wkv_hbm, mq_hbm, mkv_hbm,
    wq_out, wkv_out, mq_out, mkv_out,
    mq_ref, mkv_ref, peak_ref, uq_ref, ukv_ref, wq_ref, wkv_ref, new_q, new_kv, load_sem, sem,
):
    loads = [
        pltpu.make_async_copy(src, dst, load_sem.at[n])
        for n, (src, dst) in enumerate(
            (
                (peak_hbm, peak_ref), (uq_hbm, uq_ref), (wq_hbm, wq_ref), (ukv_hbm, ukv_ref), (wkv_hbm, wkv_ref),
                (mq_hbm, mq_ref), (mkv_hbm, mkv_ref),
            )
        )
    ]
    for load in loads:
        load.start()
    copies = [
        pltpu.make_async_copy(src, dst, sem.at[n])
        for n, (src, dst) in enumerate(
            ((mq_ref, mq_out), (mkv_ref, mkv_out), (new_q, wq_out), (new_kv, wkv_out))
        )
    ]
    qw, heads = wq_ref.shape
    for load in loads[:3]:
        load.wait()
    clip = jnp.minimum(1.0, clip_limit / peak_ref[...])
    root = jnp.sqrt(clip)
    scale = rms_match * math.sqrt(max(QRANK, QDIM))
    for low in range(0, qw, QDIM):
        for start, stop, factor in ((low, low + NOPE, root), (low + NOPE, low + QDIM, clip)):
            wide = wq_ref[start:stop, :].astype(F32)
            fresh = wide - learn_rate * (scale * uq_ref[start:stop, :].astype(F32) + weight_decay * wide)
            new_q[start:stop, :] = (fresh * factor).astype(BF)
    copies[2].start()
    for load in loads[5:]:
        load.wait()
    copies[0].start()
    copies[1].start()
    for load in loads[3:5]:
        load.wait()
    scale = rms_match * math.sqrt(max(KVRANK, KVDIM))
    wide = wkv_ref[...].astype(F32)
    fresh = wide - learn_rate * (scale * ukv_ref[...].astype(F32) + weight_decay * wide)
    root_rows = jnp.transpose(jnp.broadcast_to(root, (NOPE, heads)))
    new_kv[:, :NOPE] = (fresh[:, :NOPE] * root_rows).astype(BF)
    new_kv[:, NOPE:] = fresh[:, NOPE:].astype(BF)
    copies[3].start()
    for copy in copies:
        copy.wait()


def local(q_weight, kv_weight, q_grad, kv_grad, q_moment, kv_moment, logit_part, slot_table):
    heads = q_weight.shape[0]
    total = q_moment.shape[0]
    qw = q_weight.shape[3]
    kvw = kv_weight.shape[3]
    lanes = 128
    halves = kvw // lanes
    parts = qw // QDIM
    hbm = pl.BlockSpec(memory_space=pl.ANY)
    split = kv_grad.reshape(heads, 2, halves, lanes)
    travel = [pltpu.VMEM((total, width), BF) for _ in range(8) for width in CHUNKS]
    uq, ukv, mq, mkv, peak = pl.pallas_call(
        kernel,
        out_shape=(
            jax.ShapeDtypeStruct((qw, heads), BF),
            jax.ShapeDtypeStruct((heads, kvw), BF),
            jax.ShapeDtypeStruct((qw, total), F32),
            jax.ShapeDtypeStruct((halves * total, lanes), F32),
            jax.ShapeDtypeStruct((1, heads), F32),
        ),
        in_specs=[hbm] * 6,
        out_specs=tuple([hbm] * 5),
        scratch_shapes=[
            pltpu.VMEM((1, heads), jnp.int32),
            pltpu.VMEM((1, heads), F32),
            pltpu.VMEM((2, qw, heads), BF),
            pltpu.VMEM((2 * halves * heads, lanes), BF),
            pltpu.VMEM((qw, total), F32),
            pltpu.VMEM((halves * total, lanes), F32),
            pltpu.VMEM((qw, heads), BF),
            pltpu.VMEM((heads, kvw), BF),
            pltpu.VMEM((qw, total), F32),
            pltpu.VMEM((halves * total, lanes), F32),
            pltpu.VMEM((1, heads), F32),
            pltpu.VMEM((qw, heads), BF),
            pltpu.VMEM((heads, kvw), BF),
            pltpu.VMEM((heads, kvw), BF),
            pltpu.VMEM((heads, kvw), BF),
            pltpu.VMEM((Q_PAD, heads), BF),
            pltpu.VMEM((total, heads), BF),
            pltpu.VMEM((total, heads), BF),
            pltpu.VMEM((total, total), BF),
            *travel,
            pltpu.VMEM((qw, total), BF),
            pltpu.VMEM((qw, total), BF),
            pltpu.VMEM((total, kvw), BF),
            pltpu.VMEM((total, kvw), BF),
            pltpu.VMEM((QDIM, 2 * parts * total), BF),
            pltpu.VMEM((KVDIM, 2 * total), BF),
            pltpu.VMEM((Q_PAD, total), BF),
            pltpu.VMEM((GZ, 1, heads), F32),
            pltpu.VMEM((1, heads), F32),
            pltpu.VMEM((GYX, 1, heads), F32),
            pltpu.VMEM((1, heads), F32),
            pltpu.VMEM((1, heads), F32),
            pltpu.SemaphoreType.DMA((6,)),
            pltpu.SemaphoreType.DMA((5,)),
            pltpu.SemaphoreType.DMA((7,)),
            pltpu.SemaphoreType.DMA((7,)),
            pltpu.SemaphoreType.DMA((2,)),
            pltpu.SemaphoreType.DMA((2,)),
            *[pltpu.SemaphoreType.DMA((3,)) for _ in range(8)],
        ],
        compiler_params=pltpu.CompilerParams(
            collective_id=0, has_side_effects=True, vmem_limit_bytes=VMEM_LIMIT
        ),
        cost_estimate=pl.CostEstimate(flops=4_000_000_000, bytes_accessed=4_000_000, transcendentals=0),
    )(
        slot_table.reshape(1, heads),
        logit_part.reshape(1, heads),
        jnp.transpose(q_grad.reshape(heads, 2, qw), (1, 2, 0)),
        jnp.transpose(split, (0, 2, 1, 3)).reshape(2 * halves * heads, lanes),
        jnp.transpose(q_moment.reshape(total, qw)),
        kv_moment.reshape(halves * total, lanes),
    )
    wq, wkv, mq, mkv = pl.pallas_call(
        finish,
        out_shape=(
            jax.ShapeDtypeStruct((qw, heads), BF),
            jax.ShapeDtypeStruct((heads, kvw), BF),
            jax.ShapeDtypeStruct((qw, total), F32),
            jax.ShapeDtypeStruct((halves * total, lanes), F32),
        ),
        in_specs=[hbm] * 7,
        out_specs=tuple([hbm] * 4),
        scratch_shapes=[
            pltpu.VMEM((qw, total), F32),
            pltpu.VMEM((halves * total, lanes), F32),
            pltpu.VMEM((1, heads), F32),
            pltpu.VMEM((qw, heads), BF),
            pltpu.VMEM((heads, kvw), BF),
            pltpu.VMEM((qw, heads), BF),
            pltpu.VMEM((heads, kvw), BF),
            pltpu.VMEM((qw, heads), BF),
            pltpu.VMEM((heads, kvw), BF),
            pltpu.SemaphoreType.DMA((7,)),
            pltpu.SemaphoreType.DMA((4,)),
        ],
        compiler_params=pltpu.CompilerParams(vmem_limit_bytes=VMEM_LIMIT),
        cost_estimate=pl.CostEstimate(flops=4_000_000, bytes_accessed=4_000_000, transcendentals=0),
    )(peak, uq, ukv, jnp.transpose(q_weight.reshape(heads, qw)), kv_weight.reshape(heads, kvw), mq, mkv)
    return (
        jnp.transpose(wq).reshape(q_weight.shape),
        wkv.reshape(kv_weight.shape),
        jnp.transpose(mq).reshape(q_moment.shape),
        mkv.reshape(kv_moment.shape),
    )


def solution(mesh):
    in_specs = (
        P(None, "dp", "ctx", None),
        P(None, "dp", "ctx", None),
        P("ctx", None, "dp", None, None),
        P("ctx", None, "dp", None, None),
        P(None, "ctx", "dp", None),
        P(None, "ctx", "dp", None),
        P("dp", "ctx", None),
        P(),
    )
    out_specs = (
        P(None, "dp", "ctx", None),
        P(None, "dp", "ctx", None),
        P(None, "ctx", "dp", None),
        P(None, "ctx", "dp", None),
    )
    return jax.shard_map(local, mesh=mesh, in_specs=in_specs, out_specs=out_specs, check_vma=False)
```

```python
import math

import jax
import jax.numpy as jnp
from jax import lax
from jax.experimental import pallas as pl
from jax.experimental.pallas import tpu as pltpu
from jax.sharding import PartitionSpec as P

NOPE = 128
ITERS = 5
QDIM = 192
KVDIM = 256

GY = 4
GX = 4
GZ = 16
GYX = GY * GX
QRANK = 1536
KVRANK = 512

newton_a = 3.4445
newton_b = -4.775
newton_c = 2.0315
momentum_rate = 0.95
learn_rate = 2.0
weight_decay = 0.1
rms_match = 0.2
clip_limit = 100.0
norm_eps = 1e-06

MESH = pl.DeviceIdType.MESH
BF = jnp.bfloat16
F32 = jnp.float32

CHUNKS = (256, 384, 256)
Q_CUTS = ((0, 256), (256, 640))
Q_PAD = 640
Z_FIRST = 1
VMEM_LIMIT = 62 * 1024 * 1024


def nt(a, b):
    return lax.dot_general(a, b, (((1,), (1,)), ((), ())), preferred_element_type=F32)


def nn(a, b):
    return lax.dot_general(a, b, (((1,), (0,)), ((), ())), preferred_element_type=F32)


def tn(a, b):
    return lax.dot_general(a, b, (((0,), (0,)), ((), ())), preferred_element_type=F32)


def one_hot(mask):
    return jnp.where(mask, 1.0, 0.0).astype(BF)


def kernel(
    slot_hbm, logit_hbm, gq_hbm, gkv_hbm, mq_hbm, mkv_hbm,
    uq_hbm, ukv_hbm, mq_new_hbm, mkv_new_hbm, peak_hbm,
    slot_ref, logit_ref, gq_ref, gkv_ref, mq_ref, mkv_ref,
    uq_out, ukv_out, mq_out, mkv_out, peak_out,
    xq, xkv, okv, skv, qs, place, pick, swap,
    fsa0, fsa1, fsa2, fra0, fra1, fra2, fsb0, fsb1, fsb2, frb0, frb1, frb2,
    bsa0, bsa1, bsa2, bra0, bra1, bra2, bsb0, bsb1, bsb2, brb0, brb1, brb2,
    mbq, mpq, mbkv, mpkv, xt, xk, xf,
    lz, lm, ly, lc, lp,
    load_sem, store_sem, core_send, core_recv, log_send, log_recv, fa_send, fa_recv, fb_send, fb_recv,
    ba_send, ba_recv, bb_send, bb_recv,
):
    fsa, fra, fsb, frb = (fsa0, fsa1, fsa2), (fra0, fra1, fra2), (fsb0, fsb1, fsb2), (frb0, frb1, frb2)
    bsa, bra, bsb, brb = (bsa0, bsa1, bsa2), (bra0, bra1, bra2), (bsb0, bsb1, bsb2), (brb0, brb1, brb2)
    me = lax.axis_index("dp")
    core = lax.axis_index("ctx")
    other = 1 - core
    z = lax.rem(me, GZ)
    yx = lax.div(me, GZ)
    y = lax.div(yx, GX)
    x = lax.rem(yx, GX)
    total = GZ * GYX
    heads = slot_ref.shape[1]
    qw = mq_ref.shape[0]
    lanes = mkv_ref.shape[1]
    halves = KVDIM // lanes

    def z_peer(i):
        j = i + 1
        step = GZ // 2 - j // 2
        sign = 1 - 2 * (j % 2)
        return lax.rem(z + sign * step + GZ, GZ)

    def yx_peer(i):
        j = GYX - 1 - i
        return lax.rem(y + j // GX, GY) * GX + lax.rem(x + j % GX, GX)

    def z_dev(zt):
        return (yx * GZ + zt, core)

    def yx_dev(yxt):
        return (yxt * GZ + z, core)

    barrier = pltpu.get_barrier_semaphore()

    def greet_z(i, carry):
        pl.semaphore_signal(barrier, inc=1, device_id=z_dev(z_peer(i)), device_id_type=MESH)
        return carry

    def greet_yx(i, carry):
        pl.semaphore_signal(barrier, inc=1, device_id=yx_dev(yx_peer(i)), device_id_type=MESH)
        return carry

    lax.fori_loop(0, GZ - 1, greet_z, 0)
    lax.fori_loop(0, GYX - 1, greet_yx, 0)
    pl.semaphore_signal(barrier, inc=1, device_id=(me, other), device_id_type=MESH)

    loads = [
        pltpu.make_async_copy(src, dst, load_sem.at[n])
        for n, (src, dst) in enumerate(
            (
                (gq_hbm, gq_ref), (gkv_hbm, gkv_ref), (mq_hbm, mq_ref), (mkv_hbm, mkv_ref),
                (slot_hbm, slot_ref), (logit_hbm, logit_ref),
            )
        )
    ]
    stores = [
        pltpu.make_async_copy(src, dst, store_sem.at[n])
        for n, (src, dst) in enumerate(
            (
                (uq_out, uq_hbm), (ukv_out, ukv_hbm), (mq_out, mq_new_hbm), (mkv_out, mkv_new_hbm),
                (peak_out, peak_hbm),
            )
        )
    ]
    for n in (4, 1, 0, 5, 2, 3):
        loads[n].start()

    loads[4].wait()
    rows = lax.broadcasted_iota(jnp.int32, (total, heads), 0)
    place[...] = one_hot(slot_ref[...] == (rows % GYX) * GZ + rows // GYX)
    pick[...] = one_hot(slot_ref[...] == rows)
    rows = lax.broadcasted_iota(jnp.int32, (total, total), 0)
    cols = lax.broadcasted_iota(jnp.int32, (total, total), 1)
    swap[...] = one_hot(cols == (rows % GZ) * GYX + rows // GZ)
    qs[qw:, :] = jnp.zeros((Q_PAD - qw, heads), BF)
    xf[qw:, :] = jnp.zeros((Q_PAD - qw, total), BF)

    def pick_rows(dst, half):
        cols = lax.broadcasted_iota(jnp.int32, (heads, 2 * halves * heads), 1)
        rows = lax.broadcasted_iota(jnp.int32, (heads, 2 * halves * heads), 0)
        offset = cols - 2 * halves * rows
        for t in range(halves):
            dst[:, t * lanes : (t + 1) * lanes] = nn(one_hot(offset == 2 * t + half), gkv_ref[...]).astype(BF)

    loads[1].wait()
    loads[0].wait()
    loads[5].wait()

    pl.semaphore_wait(barrier, GZ - 1 + GYX - 1 + 1)

    def to_core(src, dst, slot):
        return pltpu.make_async_remote_copy(
            src_ref=src, dst_ref=dst, send_sem=core_send.at[slot], recv_sem=core_recv.at[slot],
            device_id=(me, other), device_id_type=MESH,
        )

    spans = tuple(slice(low, min(high, qw)) for low, high in Q_CUTS)
    core_q = [to_core(gq_ref.at[other, span], xq.at[span], n) for n, span in enumerate(spans)]
    core_kv = to_core(okv, xkv, 2)
    for copy in core_q[::-1]:
        copy.start()
    pick_rows(okv, other)
    core_kv.start()

    def send_z(src, dst, send_sem, recv_sem, zt):
        pltpu.make_async_remote_copy(
            src_ref=src.at[pl.ds(pl.multiple_of(zt * GYX, GYX), GYX)],
            dst_ref=dst.at[pl.ds(pl.multiple_of(z * GYX, GYX), GYX)],
            send_sem=send_sem, recv_sem=recv_sem,
            device_id=z_dev(zt), device_id_type=MESH,
        ).start()

    def keep_z(src, dst):
        mine = pl.ds(pl.multiple_of(z * GYX, GYX), GYX)
        dst[mine, :] = src[mine, :]

    def all_z(src, dst, send_sem, recv_sem):
        def body(i, carry):
            send_z(src, dst, send_sem, recv_sem, z_peer(i))
            return carry

        lax.fori_loop(0, GZ - 1, body, 0)
        keep_z(src, dst)

    def all_yx(src, dst, send_sem, recv_sem):
        def body(i, carry):
            yxt = yx_peer(i)
            pltpu.make_async_remote_copy(
                src_ref=src.at[pl.ds(pl.multiple_of(yxt * GZ, GZ), GZ)],
                dst_ref=dst.at[pl.ds(pl.multiple_of(yx * GZ, GZ), GZ)],
                send_sem=send_sem, recv_sem=recv_sem,
                device_id=yx_dev(yxt), device_id_type=MESH,
            ).start()
            return carry

        lax.fori_loop(0, GYX - 1, body, 0)
        mine = pl.ds(pl.multiple_of(yx * GZ, GZ), GZ)
        dst[mine, :] = src[mine, :]

    def wait_rows(buf, count, sem):
        view = buf.at[pl.ds(0, count)]
        pltpu.make_async_copy(view, view, sem).wait()

    def wait_z(buf, sem):
        wait_rows(buf, (GZ - 1) * GYX, sem)

    def wait_yx(buf, sem):
        wait_rows(buf, (GYX - 1) * GZ, sem)

    def logits_z(i, carry):
        pltpu.make_async_remote_copy(
            src_ref=logit_ref, dst_ref=lz.at[z], send_sem=log_send.at[0], recv_sem=log_recv.at[0],
            device_id=z_dev(z_peer(i)), device_id_type=MESH,
        ).start()
        return carry

    def logits_yx(i, carry):
        pltpu.make_async_remote_copy(
            src_ref=lm, dst_ref=ly.at[yx], send_sem=log_send.at[1], recv_sem=log_recv.at[1],
            device_id=yx_dev(yx_peer(i)), device_id_type=MESH,
        ).start()
        return carry

    lax.fori_loop(0, GZ - 1, logits_z, 0)
    lz[z] = logit_ref[...]

    for n in (1, 0):
        core_q[n].wait()
        low, high = Q_CUTS[n]
        span = spans[n]
        qs[span, :] = (gq_ref[core, span].astype(F32) + xq[span, :].astype(F32)).astype(BF)
        if n == Z_FIRST:
            fsa[n][...] = nt(place[...], qs[low:high, :]).astype(BF)
            all_z(fsa[n], fra[n], fa_send.at[n], fa_recv.at[n])
        else:
            fsa[n][...] = nt(pick[...], qs[low:high, :]).astype(BF)
            all_yx(fsa[n], fra[n], fa_send.at[n], fa_recv.at[n])
    pick_rows(skv, core)
    core_kv.wait()
    kvs = (skv[...].astype(F32) + xkv[...].astype(F32)).astype(BF)
    fsa[2][...] = nn(pick[...], kvs).astype(BF)
    all_yx(fsa[2], fra[2], fa_send.at[2], fa_recv.at[2])

    def second_leg(n, src, mid, dst, first_recv, send_sem, recv_sem):
        wait_rows(src, (GZ - 1) * GYX, first_recv)
        mid[...] = nn(swap[...], src[...]).astype(BF)
        leg = all_yx if n == Z_FIRST else all_z
        leg(mid, dst, send_sem, recv_sem)

    def forward_mid(n):
        second_leg(n, fra[n], fsb[n], frb[n], fa_recv.at[n], fb_send.at[n], fb_recv.at[n])

    loads[2].wait()
    loads[3].wait()
    forward_mid(0)
    forward_mid(2)
    forward_mid(1)

    view = lz.at[pl.ds(0, GZ - 1)]
    pltpu.make_async_copy(view, view, log_recv.at[0]).wait()
    lm[...] = jnp.max(lz[...], axis=0)
    lax.fori_loop(0, GYX - 1, logits_yx, 0)
    ly[yx] = lm[...]

    core_mq = [to_core(mbq.at[span], mpq.at[span], 3 + n) for n, span in enumerate(spans)]
    for n in (1, 0):
        low, high = Q_CUTS[n]
        wait_yx(frb[n], fb_recv.at[n])
        span = spans[n]
        real = min(high, qw) - low
        size = high - low
        if n == Z_FIRST:
            eye = one_hot(
                lax.broadcasted_iota(jnp.int32, (real, size), 0) == lax.broadcasted_iota(jnp.int32, (real, size), 1)
            )
            arrived = nt(eye, frb[n][...])
        else:
            arrived = tn(frb[n][...], swap[...])[:real, :]
        fresh = momentum_rate * mq_ref[span, :] + arrived
        mbq[span, :] = fresh.astype(BF)
        core_mq[n].start()
        mq_out[span, :] = fresh
    stores[2].start()

    def grams(ref):
        return sum(nt(ref[j * QDIM : (j + 1) * QDIM, :], ref[j * QDIM : (j + 1) * QDIM, :]) for j in range(parts))

    def mix(gram):
        return (newton_b * gram.astype(F32) + newton_c * nn(gram, gram)).astype(BF)

    def newton(ref, width):
        mixer = mix(nt(ref[...], ref[...]).astype(BF))
        for low in range(0, width, total):
            piece = ref[:, low : low + total]
            yield low, (newton_a * piece.astype(F32) + nn(mixer, piece)).astype(BF)

    parts = qw // QDIM
    raw = grams(mbq)
    for n in (1, 0):
        core_mq[n].wait()
    raw = raw + grams(mpq)
    diagonal = lax.broadcasted_iota(jnp.int32, raw.shape, 0) == lax.broadcasted_iota(jnp.int32, raw.shape, 1)
    squares = jnp.sum(jnp.where(diagonal, raw, 0.0), keepdims=True)
    scale = 1.0 / (jnp.sqrt(squares) + norm_eps)
    mixer = mix((raw * scale * scale).astype(BF))
    for j in range(parts):
        band = slice(j * QDIM, (j + 1) * QDIM)
        for lane, ref in ((j * total, mq_out), ((parts + j) * total, mpq)):
            piece = (ref[band, :].astype(F32) * scale).astype(BF)
            xt[:, lane : lane + total] = (newton_a * piece.astype(F32) + nn(mixer, piece)).astype(BF)
    for iteration in range(1, ITERS - 1):
        for low, piece in newton(xt, 2 * parts * total):
            xt[:, low : low + total] = piece
    for low, piece in newton(xt, parts * total):
        j = low // total
        xf[j * QDIM : (j + 1) * QDIM, :] = piece

    same = one_hot(
        lax.broadcasted_iota(jnp.int32, (total, total), 0) == lax.broadcasted_iota(jnp.int32, (total, total), 1)
    )
    for n in (1, 0):
        low, high = Q_CUTS[n]
        if n == Z_FIRST:
            bsa[n][...] = nt(swap[...], xf[low:high, :]).astype(BF)
            all_z(bsa[n], bra[n], ba_send.at[n], ba_recv.at[n])
        else:
            bsa[n][...] = nt(same, xf[low:high, :]).astype(BF)
            all_yx(bsa[n], bra[n], ba_send.at[n], ba_recv.at[n])

    def back_mid(n):
        second_leg(n, bra[n], bsb[n], brb[n], ba_recv.at[n], bb_send.at[n], bb_recv.at[n])

    wait_yx(frb[2], fb_recv.at[2])
    arrived = nn(swap[...], frb[2][...])
    for t in range(halves):
        band = slice(t * lanes, (t + 1) * lanes)
        picked = pl.ds(t, total, stride=halves)
        fresh = momentum_rate * mkv_ref[picked, :] + arrived[:, band]
        mkv_out[picked, :] = fresh
        mbkv[:, band] = fresh.astype(BF)
    core_mkv = to_core(mbkv, mpkv, 5)
    core_mkv.start()
    stores[3].start()
    ours = mkv_out[...]
    squares = jnp.sum(ours * ours, keepdims=True)
    eye = one_hot(
        lax.broadcasted_iota(jnp.int32, (lanes, lanes), 0) == lax.broadcasted_iota(jnp.int32, (lanes, lanes), 1)
    )
    core_mkv.wait()
    theirs = mpkv[...].astype(F32)
    squares = squares + jnp.sum(theirs * theirs, keepdims=True)
    scale = 1.0 / (jnp.sqrt(squares) + norm_eps)
    for t in range(halves):
        band = slice(t * lanes, (t + 1) * lanes)
        ours = mkv_out[pl.ds(t, total, stride=halves), :]
        xk[band, :total] = nt(eye, (ours * scale).astype(BF)).astype(BF)
        xk[band, total:] = nt(eye, (theirs[:, band] * scale).astype(BF)).astype(BF)
    for iteration in range(ITERS - 1):
        if iteration == 2:
            back_mid(0)
        for low, piece in newton(xk, 2 * total):
            xk[:, low : low + total] = piece
    for low, piece in newton(xk, total):
        bsa[2][...] = nt(same, piece).astype(BF)
    all_yx(bsa[2], bra[2], ba_send.at[2], ba_recv.at[2])

    view = ly.at[pl.ds(0, GYX - 1)]
    pltpu.make_async_copy(view, view, log_recv.at[1]).wait()
    lc[...] = jnp.max(ly[...], axis=0)
    core_peak = to_core(lc, lp, 6)
    core_peak.start()
    core_peak.wait()
    peak_out[...] = jnp.maximum(lc[...], lp[...])
    stores[4].start()

    back_mid(2)
    back_mid(1)

    for n, (low, high) in enumerate(Q_CUTS):
        wait_yx(brb[n], bb_recv.at[n])
        real = min(high, qw) - low
        order = pick if n == Z_FIRST else place
        uq_out[spans[n], :] = tn(brb[n][...], order[...])[:real, :].astype(BF)
    stores[0].start()
    for n in range(3):
        wait_z(fsa[n], fa_send.at[n])
        wait_z(bsa[n], ba_send.at[n])
        wait_yx(fsb[n], fb_send.at[n])
    view = lz.at[pl.ds(0, GZ - 1)]
    pltpu.make_async_copy(view, view, log_send.at[0]).wait()
    view = ly.at[pl.ds(0, GYX - 1)]
    pltpu.make_async_copy(view, view, log_send.at[1]).wait()
    wait_yx(brb[2], bb_recv.at[2])
    ukv_out[...] = tn(place[...], brb[2][...]).astype(BF)
    stores[1].start()
    for n in range(3):
        wait_yx(bsb[n], bb_send.at[n])
    for store in stores:
        store.wait()


def finish(
    peak_hbm, uq_hbm, ukv_hbm, wq_hbm, wkv_hbm, mq_hbm, mkv_hbm,
    wq_out, wkv_out, mq_out, mkv_out,
    mq_ref, mkv_ref, peak_ref, uq_ref, ukv_ref, wq_ref, wkv_ref, new_q, new_kv, load_sem, sem,
):
    loads = [
        pltpu.make_async_copy(src, dst, load_sem.at[n])
        for n, (src, dst) in enumerate(
            (
                (peak_hbm, peak_ref), (uq_hbm, uq_ref), (wq_hbm, wq_ref), (ukv_hbm, ukv_ref), (wkv_hbm, wkv_ref),
                (mq_hbm, mq_ref), (mkv_hbm, mkv_ref),
            )
        )
    ]
    for load in loads:
        load.start()
    copies = [
        pltpu.make_async_copy(src, dst, sem.at[n])
        for n, (src, dst) in enumerate(
            ((mq_ref, mq_out), (mkv_ref, mkv_out), (new_q, wq_out), (new_kv, wkv_out))
        )
    ]
    qw, heads = wq_ref.shape
    for load in loads[:3]:
        load.wait()
    clip = jnp.minimum(1.0, clip_limit / peak_ref[...])
    root = jnp.sqrt(clip)
    scale = rms_match * math.sqrt(max(QRANK, QDIM))
    for low in range(0, qw, QDIM):
        for start, stop, factor in ((low, low + NOPE, root), (low + NOPE, low + QDIM, clip)):
            wide = wq_ref[start:stop, :].astype(F32)
            fresh = wide - learn_rate * (scale * uq_ref[start:stop, :].astype(F32) + weight_decay * wide)
            new_q[start:stop, :] = (fresh * factor).astype(BF)
    copies[2].start()
    for load in loads[5:]:
        load.wait()
    copies[0].start()
    copies[1].start()
    for load in loads[3:5]:
        load.wait()
    scale = rms_match * math.sqrt(max(KVRANK, KVDIM))
    wide = wkv_ref[...].astype(F32)
    fresh = wide - learn_rate * (scale * ukv_ref[...].astype(F32) + weight_decay * wide)
    root_rows = jnp.transpose(jnp.broadcast_to(root, (NOPE, heads)))
    new_kv[:, :NOPE] = (fresh[:, :NOPE] * root_rows).astype(BF)
    new_kv[:, NOPE:] = fresh[:, NOPE:].astype(BF)
    copies[3].start()
    for copy in copies:
        copy.wait()


def local(q_weight, kv_weight, q_grad, kv_grad, q_moment, kv_moment, logit_part, slot_table):
    heads = q_weight.shape[0]
    total = q_moment.shape[0]
    qw = q_weight.shape[3]
    kvw = kv_weight.shape[3]
    lanes = 128
    halves = kvw // lanes
    parts = qw // QDIM
    hbm = pl.BlockSpec(memory_space=pl.ANY)
    split = kv_grad.reshape(heads, 2, halves, lanes)
    travel = [pltpu.VMEM((total, width), BF) for _ in range(8) for width in CHUNKS]
    uq, ukv, mq, mkv, peak = pl.pallas_call(
        kernel,
        out_shape=(
            jax.ShapeDtypeStruct((qw, heads), BF),
            jax.ShapeDtypeStruct((heads, kvw), BF),
            jax.ShapeDtypeStruct((qw, total), F32),
            jax.ShapeDtypeStruct((halves * total, lanes), F32),
            jax.ShapeDtypeStruct((1, heads), F32),
        ),
        in_specs=[hbm] * 6,
        out_specs=tuple([hbm] * 5),
        scratch_shapes=[
            pltpu.VMEM((1, heads), jnp.int32),
            pltpu.VMEM((1, heads), F32),
            pltpu.VMEM((2, qw, heads), BF),
            pltpu.VMEM((2 * halves * heads, lanes), BF),
            pltpu.VMEM((qw, total), F32),
            pltpu.VMEM((halves * total, lanes), F32),
            pltpu.VMEM((qw, heads), BF),
            pltpu.VMEM((heads, kvw), BF),
            pltpu.VMEM((qw, total), F32),
            pltpu.VMEM((halves * total, lanes), F32),
            pltpu.VMEM((1, heads), F32),
            pltpu.VMEM((qw, heads), BF),
            pltpu.VMEM((heads, kvw), BF),
            pltpu.VMEM((heads, kvw), BF),
            pltpu.VMEM((heads, kvw), BF),
            pltpu.VMEM((Q_PAD, heads), BF),
            pltpu.VMEM((total, heads), BF),
            pltpu.VMEM((total, heads), BF),
            pltpu.VMEM((total, total), BF),
            *travel,
            pltpu.VMEM((qw, total), BF),
            pltpu.VMEM((qw, total), BF),
            pltpu.VMEM((total, kvw), BF),
            pltpu.VMEM((total, kvw), BF),
            pltpu.VMEM((QDIM, 2 * parts * total), BF),
            pltpu.VMEM((KVDIM, 2 * total), BF),
            pltpu.VMEM((Q_PAD, total), BF),
            pltpu.VMEM((GZ, 1, heads), F32),
            pltpu.VMEM((1, heads), F32),
            pltpu.VMEM((GYX, 1, heads), F32),
            pltpu.VMEM((1, heads), F32),
            pltpu.VMEM((1, heads), F32),
            pltpu.SemaphoreType.DMA((6,)),
            pltpu.SemaphoreType.DMA((5,)),
            pltpu.SemaphoreType.DMA((7,)),
            pltpu.SemaphoreType.DMA((7,)),
            pltpu.SemaphoreType.DMA((2,)),
            pltpu.SemaphoreType.DMA((2,)),
            *[pltpu.SemaphoreType.DMA((3,)) for _ in range(8)],
        ],
        compiler_params=pltpu.CompilerParams(
            collective_id=0, has_side_effects=True, vmem_limit_bytes=VMEM_LIMIT
        ),
        cost_estimate=pl.CostEstimate(flops=4_000_000_000, bytes_accessed=4_000_000, transcendentals=0),
    )(
        slot_table.reshape(1, heads),
        logit_part.reshape(1, heads),
        jnp.transpose(q_grad.reshape(heads, 2, qw), (1, 2, 0)),
        jnp.transpose(split, (0, 2, 1, 3)).reshape(2 * halves * heads, lanes),
        jnp.transpose(q_moment.reshape(total, qw)),
        kv_moment.reshape(halves * total, lanes),
    )
    wq, wkv, mq, mkv = pl.pallas_call(
        finish,
        out_shape=(
            jax.ShapeDtypeStruct((qw, heads), BF),
            jax.ShapeDtypeStruct((heads, kvw), BF),
            jax.ShapeDtypeStruct((qw, total), F32),
            jax.ShapeDtypeStruct((halves * total, lanes), F32),
        ),
        in_specs=[hbm] * 7,
        out_specs=tuple([hbm] * 4),
        scratch_shapes=[
            pltpu.VMEM((qw, total), F32),
            pltpu.VMEM((halves * total, lanes), F32),
            pltpu.VMEM((1, heads), F32),
            pltpu.VMEM((qw, heads), BF),
            pltpu.VMEM((heads, kvw), BF),
            pltpu.VMEM((qw, heads), BF),
            pltpu.VMEM((heads, kvw), BF),
            pltpu.VMEM((qw, heads), BF),
            pltpu.VMEM((heads, kvw), BF),
            pltpu.SemaphoreType.DMA((7,)),
            pltpu.SemaphoreType.DMA((4,)),
        ],
        compiler_params=pltpu.CompilerParams(vmem_limit_bytes=VMEM_LIMIT),
        cost_estimate=pl.CostEstimate(flops=4_000_000, bytes_accessed=4_000_000, transcendentals=0),
    )(peak, uq, ukv, jnp.transpose(q_weight.reshape(heads, qw)), kv_weight.reshape(heads, kvw), mq, mkv)
    return (
        jnp.transpose(wq).reshape(q_weight.shape),
        wkv.reshape(kv_weight.shape),
        jnp.transpose(mq).reshape(q_moment.shape),
        mkv.reshape(kv_moment.shape),
    )


def solution(mesh):
    in_specs = (
        P(None, "dp", "ctx", None),
        P(None, "dp", "ctx", None),
        P("ctx", None, "dp", None, None),
        P("ctx", None, "dp", None, None),
        P(None, "ctx", "dp", None),
        P(None, "ctx", "dp", None),
        P("dp", "ctx", None),
        P(),
    )
    out_specs = (
        P(None, "dp", "ctx", None),
        P(None, "dp", "ctx", None),
        P(None, "ctx", "dp", None),
        P(None, "ctx", "dp", None),
    )
    return jax.shard_map(local, mesh=mesh, in_specs=in_specs, out_specs=out_specs, check_vma=False)
```

```python
import math

import jax
import jax.numpy as jnp
from jax import lax
from jax.experimental import pallas as pl
from jax.experimental.pallas import tpu as pltpu
from jax.sharding import PartitionSpec as P

NOPE = 128
ITERS = 5
QDIM = 192
KVDIM = 256

GY = 4
GX = 4
GZ = 16
GYX = GY * GX
QRANK = 1536
KVRANK = 512

newton_a = 3.4445
newton_b = -4.775
newton_c = 2.0315
momentum_rate = 0.95
learn_rate = 2.0
weight_decay = 0.1
rms_match = 0.2
clip_limit = 100.0
norm_eps = 1e-06

MESH = pl.DeviceIdType.MESH
BF = jnp.bfloat16
F32 = jnp.float32

CHUNKS = (256, 384, 256)
Q_CUTS = ((0, 256), (256, 640))
Q_PAD = 640
Z_FIRST = 1
VMEM_LIMIT = 62 * 1024 * 1024


def nt(a, b):
    return lax.dot_general(a, b, (((1,), (1,)), ((), ())), preferred_element_type=F32)


def nn(a, b):
    return lax.dot_general(a, b, (((1,), (0,)), ((), ())), preferred_element_type=F32)


def tn(a, b):
    return lax.dot_general(a, b, (((0,), (0,)), ((), ())), preferred_element_type=F32)


def one_hot(mask):
    return jnp.where(mask, 1.0, 0.0).astype(BF)


def kernel(
    slot_hbm, logit_hbm, gq_hbm, gkv_hbm, mq_hbm, mkv_hbm,
    uq_hbm, ukv_hbm, mq_new_hbm, mkv_new_hbm, peak_hbm,
    slot_ref, logit_ref, gq_ref, gkv_ref, mq_ref, mkv_ref,
    uq_out, ukv_out, mq_out, mkv_out, peak_out,
    xq, xkv, okv, skv, qs, place, pick, swap,
    fsa0, fsa1, fsa2, fra0, fra1, fra2, fsb0, fsb1, fsb2, frb0, frb1, frb2,
    bsa0, bsa1, bsa2, bra0, bra1, bra2, bsb0, bsb1, bsb2, brb0, brb1, brb2,
    mbq, mpq, mbkv, mpkv, xt, xk, xf,
    lz, lm, ly, lc, lp,
    load_sem, store_sem, core_send, core_recv, log_send, log_recv, fa_send, fa_recv, fb_send, fb_recv,
    ba_send, ba_recv, bb_send, bb_recv,
):
    fsa, fra, fsb, frb = (fsa0, fsa1, fsa2), (fra0, fra1, fra2), (fsb0, fsb1, fsb2), (frb0, frb1, frb2)
    bsa, bra, bsb, brb = (bsa0, bsa1, bsa2), (bra0, bra1, bra2), (bsb0, bsb1, bsb2), (brb0, brb1, brb2)
    me = lax.axis_index("dp")
    core = lax.axis_index("ctx")
    other = 1 - core
    z = lax.rem(me, GZ)
    yx = lax.div(me, GZ)
    y = lax.div(yx, GX)
    x = lax.rem(yx, GX)
    total = GZ * GYX
    heads = slot_ref.shape[1]
    qw = mq_ref.shape[0]
    lanes = mkv_ref.shape[1]
    halves = KVDIM // lanes

    def z_peer(i):
        j = i + 1
        step = GZ // 2 - j // 2
        sign = 1 - 2 * (j % 2)
        return lax.rem(z + sign * step + GZ, GZ)

    def yx_peer(i):
        j = GYX - 1 - i
        return lax.rem(y + j // GX, GY) * GX + lax.rem(x + j % GX, GX)

    def z_dev(zt):
        return (yx * GZ + zt, core)

    def yx_dev(yxt):
        return (yxt * GZ + z, core)

    barrier = pltpu.get_barrier_semaphore()

    def greet_z(i, carry):
        pl.semaphore_signal(barrier, inc=1, device_id=z_dev(z_peer(i)), device_id_type=MESH)
        return carry

    def greet_yx(i, carry):
        pl.semaphore_signal(barrier, inc=1, device_id=yx_dev(yx_peer(i)), device_id_type=MESH)
        return carry

    lax.fori_loop(0, GZ - 1, greet_z, 0)
    lax.fori_loop(0, GYX - 1, greet_yx, 0)
    pl.semaphore_signal(barrier, inc=1, device_id=(me, other), device_id_type=MESH)

    loads = [
        pltpu.make_async_copy(src, dst, load_sem.at[n])
        for n, (src, dst) in enumerate(
            (
                (gq_hbm, gq_ref), (gkv_hbm, gkv_ref), (mq_hbm, mq_ref), (mkv_hbm, mkv_ref),
                (slot_hbm, slot_ref), (logit_hbm, logit_ref),
            )
        )
    ]
    stores = [
        pltpu.make_async_copy(src, dst, store_sem.at[n])
        for n, (src, dst) in enumerate(
            (
                (uq_out, uq_hbm), (ukv_out, ukv_hbm), (mq_out, mq_new_hbm), (mkv_out, mkv_new_hbm),
                (peak_out, peak_hbm),
            )
        )
    ]
    for n in (4, 1, 0, 5, 2, 3):
        loads[n].start()

    loads[4].wait()
    rows = lax.broadcasted_iota(jnp.int32, (total, heads), 0)
    place[...] = one_hot(slot_ref[...] == (rows % GYX) * GZ + rows // GYX)
    pick[...] = one_hot(slot_ref[...] == rows)
    rows = lax.broadcasted_iota(jnp.int32, (total, total), 0)
    cols = lax.broadcasted_iota(jnp.int32, (total, total), 1)
    swap[...] = one_hot(cols == (rows % GZ) * GYX + rows // GZ)
    qs[qw:, :] = jnp.zeros((Q_PAD - qw, heads), BF)
    xf[qw:, :] = jnp.zeros((Q_PAD - qw, total), BF)

    def pick_rows(dst, half):
        cols = lax.broadcasted_iota(jnp.int32, (heads, 2 * halves * heads), 1)
        rows = lax.broadcasted_iota(jnp.int32, (heads, 2 * halves * heads), 0)
        offset = cols - 2 * halves * rows
        for t in range(halves):
            dst[:, t * lanes : (t + 1) * lanes] = nn(one_hot(offset == 2 * t + half), gkv_ref[...]).astype(BF)

    loads[1].wait()
    loads[0].wait()
    loads[5].wait()

    pl.semaphore_wait(barrier, GZ - 1 + GYX - 1 + 1)

    def to_core(src, dst, slot):
        return pltpu.make_async_remote_copy(
            src_ref=src, dst_ref=dst, send_sem=core_send.at[slot], recv_sem=core_recv.at[slot],
            device_id=(me, other), device_id_type=MESH,
        )

    spans = tuple(slice(low, min(high, qw)) for low, high in Q_CUTS)
    core_q = [to_core(gq_ref.at[other, span], xq.at[span], n) for n, span in enumerate(spans)]
    core_kv = to_core(okv, xkv, 2)
    for copy in core_q[::-1]:
        copy.start()
    pick_rows(okv, other)
    core_kv.start()

    def send_z(src, dst, send_sem, recv_sem, zt):
        pltpu.make_async_remote_copy(
            src_ref=src.at[pl.ds(pl.multiple_of(zt * GYX, GYX), GYX)],
            dst_ref=dst.at[pl.ds(pl.multiple_of(z * GYX, GYX), GYX)],
            send_sem=send_sem, recv_sem=recv_sem,
            device_id=z_dev(zt), device_id_type=MESH,
        ).start()

    def keep_z(src, dst):
        mine = pl.ds(pl.multiple_of(z * GYX, GYX), GYX)
        dst[mine, :] = src[mine, :]

    def all_z(src, dst, send_sem, recv_sem):
        def body(i, carry):
            send_z(src, dst, send_sem, recv_sem, z_peer(i))
            return carry

        lax.fori_loop(0, GZ - 1, body, 0)
        keep_z(src, dst)

    def all_yx(src, dst, send_sem, recv_sem):
        def body(i, carry):
            yxt = yx_peer(i)
            pltpu.make_async_remote_copy(
                src_ref=src.at[pl.ds(pl.multiple_of(yxt * GZ, GZ), GZ)],
                dst_ref=dst.at[pl.ds(pl.multiple_of(yx * GZ, GZ), GZ)],
                send_sem=send_sem, recv_sem=recv_sem,
                device_id=yx_dev(yxt), device_id_type=MESH,
            ).start()
            return carry

        lax.fori_loop(0, GYX - 1, body, 0)
        mine = pl.ds(pl.multiple_of(yx * GZ, GZ), GZ)
        dst[mine, :] = src[mine, :]

    def wait_rows(buf, count, sem):
        view = buf.at[pl.ds(0, count)]
        pltpu.make_async_copy(view, view, sem).wait()

    def wait_z(buf, sem):
        wait_rows(buf, (GZ - 1) * GYX, sem)

    def wait_yx(buf, sem):
        wait_rows(buf, (GYX - 1) * GZ, sem)

    def logits_z(i, carry):
        pltpu.make_async_remote_copy(
            src_ref=logit_ref, dst_ref=lz.at[z], send_sem=log_send.at[0], recv_sem=log_recv.at[0],
            device_id=z_dev(z_peer(i)), device_id_type=MESH,
        ).start()
        return carry

    def logits_yx(i, carry):
        pltpu.make_async_remote_copy(
            src_ref=lm, dst_ref=ly.at[yx], send_sem=log_send.at[1], recv_sem=log_recv.at[1],
            device_id=yx_dev(yx_peer(i)), device_id_type=MESH,
        ).start()
        return carry

    lax.fori_loop(0, GZ - 1, logits_z, 0)
    lz[z] = logit_ref[...]

    for n in (1, 0):
        core_q[n].wait()
        low, high = Q_CUTS[n]
        span = spans[n]
        qs[span, :] = (gq_ref[core, span].astype(F32) + xq[span, :].astype(F32)).astype(BF)
        if n == Z_FIRST:
            fsa[n][...] = nt(place[...], qs[low:high, :]).astype(BF)
            all_z(fsa[n], fra[n], fa_send.at[n], fa_recv.at[n])
        else:
            fsa[n][...] = nt(pick[...], qs[low:high, :]).astype(BF)
            all_yx(fsa[n], fra[n], fa_send.at[n], fa_recv.at[n])
    pick_rows(skv, core)
    core_kv.wait()
    kvs = (skv[...].astype(F32) + xkv[...].astype(F32)).astype(BF)
    fsa[2][...] = nn(pick[...], kvs).astype(BF)
    all_yx(fsa[2], fra[2], fa_send.at[2], fa_recv.at[2])

    def second_leg(n, src, mid, dst, first_recv, send_sem, recv_sem):
        wait_rows(src, (GZ - 1) * GYX, first_recv)
        mid[...] = nn(swap[...], src[...]).astype(BF)
        leg = all_yx if n == Z_FIRST else all_z
        leg(mid, dst, send_sem, recv_sem)

    def forward_mid(n):
        second_leg(n, fra[n], fsb[n], frb[n], fa_recv.at[n], fb_send.at[n], fb_recv.at[n])

    loads[2].wait()
    loads[3].wait()
    forward_mid(0)
    forward_mid(2)
    forward_mid(1)

    view = lz.at[pl.ds(0, GZ - 1)]
    pltpu.make_async_copy(view, view, log_recv.at[0]).wait()
    lm[...] = jnp.max(lz[...], axis=0)
    lax.fori_loop(0, GYX - 1, logits_yx, 0)
    ly[yx] = lm[...]

    squares = jnp.zeros((1, 1), F32)
    core_mq = [to_core(mbq.at[span], mpq.at[span], 3 + n) for n, span in enumerate(spans)]
    for n, (low, high) in enumerate(Q_CUTS):
        wait_yx(frb[n], fb_recv.at[n])
        span = spans[n]
        real = min(high, qw) - low
        size = high - low
        if n == Z_FIRST:
            eye = one_hot(
                lax.broadcasted_iota(jnp.int32, (real, size), 0) == lax.broadcasted_iota(jnp.int32, (real, size), 1)
            )
            arrived = nt(eye, frb[n][...])
        else:
            arrived = tn(frb[n][...], swap[...])[:real, :]
        fresh = momentum_rate * mq_ref[span, :] + arrived
        mq_out[span, :] = fresh
        mbq[span, :] = fresh.astype(BF)
        core_mq[n].start()
        squares = squares + jnp.sum(fresh * fresh, keepdims=True)
    for n, span in enumerate(spans):
        core_mq[n].wait()
        theirs = mpq[span, :].astype(F32)
        squares = squares + jnp.sum(theirs * theirs, keepdims=True)
    stores[2].start()
    scale = 1.0 / (jnp.sqrt(squares) + norm_eps)
    parts = qw // QDIM
    for j in range(parts):
        band = slice(j * QDIM, (j + 1) * QDIM)
        xt[:, j * total : (j + 1) * total] = (mq_out[band, :] * scale).astype(BF)
        lane = (parts + j) * total
        xt[:, lane : lane + total] = (mpq[band, :].astype(F32) * scale).astype(BF)

    def newton(ref, width):
        gram = nt(ref[...], ref[...]).astype(BF)
        mixer = (newton_b * gram.astype(F32) + newton_c * nn(gram, gram)).astype(BF)
        for low in range(0, width, total):
            piece = ref[:, low : low + total]
            yield low, (newton_a * piece.astype(F32) + nn(mixer, piece)).astype(BF)

    for iteration in range(ITERS - 1):
        for low, piece in newton(xt, 2 * parts * total):
            xt[:, low : low + total] = piece
    for low, piece in newton(xt, parts * total):
        j = low // total
        xf[j * QDIM : (j + 1) * QDIM, :] = piece

    same = one_hot(
        lax.broadcasted_iota(jnp.int32, (total, total), 0) == lax.broadcasted_iota(jnp.int32, (total, total), 1)
    )
    for n in (1, 0):
        low, high = Q_CUTS[n]
        if n == Z_FIRST:
            bsa[n][...] = nt(swap[...], xf[low:high, :]).astype(BF)
            all_z(bsa[n], bra[n], ba_send.at[n], ba_recv.at[n])
        else:
            bsa[n][...] = nt(same, xf[low:high, :]).astype(BF)
            all_yx(bsa[n], bra[n], ba_send.at[n], ba_recv.at[n])

    wait_yx(frb[2], fb_recv.at[2])
    arrived = nn(swap[...], frb[2][...])
    for t in range(halves):
        band = slice(t * lanes, (t + 1) * lanes)
        picked = pl.ds(t, total, stride=halves)
        fresh = momentum_rate * mkv_ref[picked, :] + arrived[:, band]
        mkv_out[picked, :] = fresh
        mbkv[:, band] = fresh.astype(BF)
    core_mkv = to_core(mbkv, mpkv, 5)
    core_mkv.start()
    stores[3].start()
    ours = mkv_out[...]
    squares = jnp.sum(ours * ours, keepdims=True)
    eye = one_hot(
        lax.broadcasted_iota(jnp.int32, (lanes, lanes), 0) == lax.broadcasted_iota(jnp.int32, (lanes, lanes), 1)
    )
    core_mkv.wait()
    theirs = mpkv[...].astype(F32)
    squares = squares + jnp.sum(theirs * theirs, keepdims=True)
    scale = 1.0 / (jnp.sqrt(squares) + norm_eps)
    for t in range(halves):
        band = slice(t * lanes, (t + 1) * lanes)
        ours = mkv_out[pl.ds(t, total, stride=halves), :]
        xk[band, :total] = nt(eye, (ours * scale).astype(BF)).astype(BF)
        xk[band, total:] = nt(eye, (theirs[:, band] * scale).astype(BF)).astype(BF)
    for iteration in range(ITERS - 1):
        for low, piece in newton(xk, 2 * total):
            xk[:, low : low + total] = piece
    for low, piece in newton(xk, total):
        bsa[2][...] = nt(same, piece).astype(BF)
    all_yx(bsa[2], bra[2], ba_send.at[2], ba_recv.at[2])

    def back_mid(n):
        second_leg(n, bra[n], bsb[n], brb[n], ba_recv.at[n], bb_send.at[n], bb_recv.at[n])

    back_mid(0)

    view = ly.at[pl.ds(0, GYX - 1)]
    pltpu.make_async_copy(view, view, log_recv.at[1]).wait()
    lc[...] = jnp.max(ly[...], axis=0)
    core_peak = to_core(lc, lp, 6)
    core_peak.start()
    core_peak.wait()
    peak_out[...] = jnp.maximum(lc[...], lp[...])
    stores[4].start()

    back_mid(2)
    back_mid(1)

    for n, (low, high) in enumerate(Q_CUTS):
        wait_yx(brb[n], bb_recv.at[n])
        real = min(high, qw) - low
        order = pick if n == Z_FIRST else place
        uq_out[spans[n], :] = tn(brb[n][...], order[...])[:real, :].astype(BF)
    stores[0].start()
    for n in range(3):
        wait_z(fsa[n], fa_send.at[n])
        wait_z(bsa[n], ba_send.at[n])
        wait_yx(fsb[n], fb_send.at[n])
    view = lz.at[pl.ds(0, GZ - 1)]
    pltpu.make_async_copy(view, view, log_send.at[0]).wait()
    view = ly.at[pl.ds(0, GYX - 1)]
    pltpu.make_async_copy(view, view, log_send.at[1]).wait()
    wait_yx(brb[2], bb_recv.at[2])
    ukv_out[...] = tn(place[...], brb[2][...]).astype(BF)
    stores[1].start()
    for n in range(3):
        wait_yx(bsb[n], bb_send.at[n])
    for store in stores:
        store.wait()


def finish(
    peak_hbm, uq_hbm, ukv_hbm, wq_hbm, wkv_hbm, mq_hbm, mkv_hbm,
    wq_out, wkv_out, mq_out, mkv_out,
    mq_ref, mkv_ref, peak_ref, uq_ref, ukv_ref, wq_ref, wkv_ref, new_q, new_kv, load_sem, sem,
):
    loads = [
        pltpu.make_async_copy(src, dst, load_sem.at[n])
        for n, (src, dst) in enumerate(
            (
                (peak_hbm, peak_ref), (uq_hbm, uq_ref), (wq_hbm, wq_ref), (ukv_hbm, ukv_ref), (wkv_hbm, wkv_ref),
                (mq_hbm, mq_ref), (mkv_hbm, mkv_ref),
            )
        )
    ]
    for load in loads[5:] + loads[:5]:
        load.start()
    copies = [
        pltpu.make_async_copy(src, dst, sem.at[n])
        for n, (src, dst) in enumerate(
            ((mq_ref, mq_out), (mkv_ref, mkv_out), (new_q, wq_out), (new_kv, wkv_out))
        )
    ]
    qw, heads = wq_ref.shape
    for n in (5, 6):
        loads[n].wait()
        copies[n - 5].start()
    for load in loads[:3]:
        load.wait()
    clip = jnp.minimum(1.0, clip_limit / peak_ref[...])
    root = jnp.sqrt(clip)
    scale = rms_match * math.sqrt(max(QRANK, QDIM))
    for low in range(0, qw, QDIM):
        for start, stop, factor in ((low, low + NOPE, root), (low + NOPE, low + QDIM, clip)):
            wide = wq_ref[start:stop, :].astype(F32)
            fresh = wide - learn_rate * (scale * uq_ref[start:stop, :].astype(F32) + weight_decay * wide)
            new_q[start:stop, :] = (fresh * factor).astype(BF)
    copies[2].start()
    for load in loads[3:5]:
        load.wait()
    scale = rms_match * math.sqrt(max(KVRANK, KVDIM))
    wide = wkv_ref[...].astype(F32)
    fresh = wide - learn_rate * (scale * ukv_ref[...].astype(F32) + weight_decay * wide)
    root_rows = jnp.transpose(jnp.broadcast_to(root, (NOPE, heads)))
    new_kv[:, :NOPE] = (fresh[:, :NOPE] * root_rows).astype(BF)
    new_kv[:, NOPE:] = fresh[:, NOPE:].astype(BF)
    copies[3].start()
    for copy in copies:
        copy.wait()


def local(q_weight, kv_weight, q_grad, kv_grad, q_moment, kv_moment, logit_part, slot_table):
    heads = q_weight.shape[0]
    total = q_moment.shape[0]
    qw = q_weight.shape[3]
    kvw = kv_weight.shape[3]
    lanes = 128
    halves = kvw // lanes
    parts = qw // QDIM
    hbm = pl.BlockSpec(memory_space=pl.ANY)
    split = kv_grad.reshape(heads, 2, halves, lanes)
    travel = [pltpu.VMEM((total, width), BF) for _ in range(8) for width in CHUNKS]
    uq, ukv, mq, mkv, peak = pl.pallas_call(
        kernel,
        out_shape=(
            jax.ShapeDtypeStruct((qw, heads), BF),
            jax.ShapeDtypeStruct((heads, kvw), BF),
            jax.ShapeDtypeStruct((qw, total), F32),
            jax.ShapeDtypeStruct((halves * total, lanes), F32),
            jax.ShapeDtypeStruct((1, heads), F32),
        ),
        in_specs=[hbm] * 6,
        out_specs=tuple([hbm] * 5),
        scratch_shapes=[
            pltpu.VMEM((1, heads), jnp.int32),
            pltpu.VMEM((1, heads), F32),
            pltpu.VMEM((2, qw, heads), BF),
            pltpu.VMEM((2 * halves * heads, lanes), BF),
            pltpu.VMEM((qw, total), F32),
            pltpu.VMEM((halves * total, lanes), F32),
            pltpu.VMEM((qw, heads), BF),
            pltpu.VMEM((heads, kvw), BF),
            pltpu.VMEM((qw, total), F32),
            pltpu.VMEM((halves * total, lanes), F32),
            pltpu.VMEM((1, heads), F32),
            pltpu.VMEM((qw, heads), BF),
            pltpu.VMEM((heads, kvw), BF),
            pltpu.VMEM((heads, kvw), BF),
            pltpu.VMEM((heads, kvw), BF),
            pltpu.VMEM((Q_PAD, heads), BF),
            pltpu.VMEM((total, heads), BF),
            pltpu.VMEM((total, heads), BF),
            pltpu.VMEM((total, total), BF),
            *travel,
            pltpu.VMEM((qw, total), BF),
            pltpu.VMEM((qw, total), BF),
            pltpu.VMEM((total, kvw), BF),
            pltpu.VMEM((total, kvw), BF),
            pltpu.VMEM((QDIM, 2 * parts * total), BF),
            pltpu.VMEM((KVDIM, 2 * total), BF),
            pltpu.VMEM((Q_PAD, total), BF),
            pltpu.VMEM((GZ, 1, heads), F32),
            pltpu.VMEM((1, heads), F32),
            pltpu.VMEM((GYX, 1, heads), F32),
            pltpu.VMEM((1, heads), F32),
            pltpu.VMEM((1, heads), F32),
            pltpu.SemaphoreType.DMA((6,)),
            pltpu.SemaphoreType.DMA((5,)),
            pltpu.SemaphoreType.DMA((7,)),
            pltpu.SemaphoreType.DMA((7,)),
            pltpu.SemaphoreType.DMA((2,)),
            pltpu.SemaphoreType.DMA((2,)),
            *[pltpu.SemaphoreType.DMA((3,)) for _ in range(8)],
        ],
        compiler_params=pltpu.CompilerParams(
            collective_id=0, has_side_effects=True, vmem_limit_bytes=VMEM_LIMIT
        ),
        cost_estimate=pl.CostEstimate(flops=4_000_000_000, bytes_accessed=4_000_000, transcendentals=0),
    )(
        slot_table.reshape(1, heads),
        logit_part.reshape(1, heads),
        jnp.transpose(q_grad.reshape(heads, 2, qw), (1, 2, 0)),
        jnp.transpose(split, (0, 2, 1, 3)).reshape(2 * halves * heads, lanes),
        jnp.transpose(q_moment.reshape(total, qw)),
        kv_moment.reshape(halves * total, lanes),
    )
    wq, wkv, mq, mkv = pl.pallas_call(
        finish,
        out_shape=(
            jax.ShapeDtypeStruct((qw, heads), BF),
            jax.ShapeDtypeStruct((heads, kvw), BF),
            jax.ShapeDtypeStruct((qw, total), F32),
            jax.ShapeDtypeStruct((halves * total, lanes), F32),
        ),
        in_specs=[hbm] * 7,
        out_specs=tuple([hbm] * 4),
        scratch_shapes=[
            pltpu.VMEM((qw, total), F32),
            pltpu.VMEM((halves * total, lanes), F32),
            pltpu.VMEM((1, heads), F32),
            pltpu.VMEM((qw, heads), BF),
            pltpu.VMEM((heads, kvw), BF),
            pltpu.VMEM((qw, heads), BF),
            pltpu.VMEM((heads, kvw), BF),
            pltpu.VMEM((qw, heads), BF),
            pltpu.VMEM((heads, kvw), BF),
            pltpu.SemaphoreType.DMA((7,)),
            pltpu.SemaphoreType.DMA((4,)),
        ],
        compiler_params=pltpu.CompilerParams(vmem_limit_bytes=VMEM_LIMIT),
        cost_estimate=pl.CostEstimate(flops=4_000_000, bytes_accessed=4_000_000, transcendentals=0),
    )(peak, uq, ukv, jnp.transpose(q_weight.reshape(heads, qw)), kv_weight.reshape(heads, kvw), mq, mkv)
    return (
        jnp.transpose(wq).reshape(q_weight.shape),
        wkv.reshape(kv_weight.shape),
        jnp.transpose(mq).reshape(q_moment.shape),
        mkv.reshape(kv_moment.shape),
    )


def solution(mesh):
    in_specs = (
        P(None, "dp", "ctx", None),
        P(None, "dp", "ctx", None),
        P("ctx", None, "dp", None, None),
        P("ctx", None, "dp", None, None),
        P(None, "ctx", "dp", None),
        P(None, "ctx", "dp", None),
        P("dp", "ctx", None),
        P(),
    )
    out_specs = (
        P(None, "dp", "ctx", None),
        P(None, "dp", "ctx", None),
        P(None, "ctx", "dp", None),
        P(None, "ctx", "dp", None),
    )
    return jax.shard_map(local, mesh=mesh, in_specs=in_specs, out_specs=out_specs, check_vma=False)
```
